32 devices in a mesh: groups: 2 (over x), gx: 16 (over z, y, core).
Axes of the slice: x: 2, y: 2, z: 4, core: 2. Of those that a mesh axis runs over, the one named last changes fastest.
Arguments:
- slab: bfloat16 [4096, 64, 256], P(('groups', 'gx')), parts along dimension 0, may hold values from -6 to 6
- factor: bfloat16 [4096, 128], P(('groups', 'gx')), parts along dimension 0, may hold values from -0.125 to 0.125
Outputs:
- gram: float32 [4096, 2048], P(('groups', 'gx')), parts along dimension 0
- core: float32 [32768, 128], P(('groups', 'gx')), parts along dimension 0
The draws below stay inside these ranges and needn't reach their ends.
There are 2 independent parts, one for each index of `groups`. The reference program is written for one: setup_inputs(seed, part) draws one part's arguments, and reference() takes and returns one part's arrays. A program takes and returns all parts, laid end to end along the dimension named above; each array names one. Nothing has to cross between parts.
All inputs are finite; a program needn't handle non-finite values.
Results may differ from the reference program's by a relative error of at most 0.0003.
Values may be sent and summed in bfloat16 or wider, within the bound.
No kernel may reach another device: no remote copies, remote signals or barrier semaphores. Data moves between devices by JAX's collectives and lax.ppermute only.
A program may use at most 128 MiB of HBM per device.

```python
import jax
import jax.numpy as jnp
from jax import lax

NX = 2048
RANK = 128
NS = 64
CELLS = 256


def block_levels(rng, shape, cuts, low, top_value):
    level = 1.0
    for position, blocks in cuts:
        steps = jax.random.uniform(jax.random.fold_in(jax.random.fold_in(rng, 6), position), (blocks,), jnp.float32, low / len(cuts), top_value / len(cuts))
        level = level * jnp.repeat(jnp.exp(steps), shape[position] // blocks).reshape((-1,) + (1,) * (len(shape) - 1 - position))
    return level


def bell_draw(rng, shape, deviation, most, split=(), dtype=jnp.bfloat16):
    loudness = block_levels(rng, shape, split, -0.22, 0.18) if split else 1.0
    drawn = jax.random.normal(rng, shape, jnp.float32) * deviation * loudness
    return jnp.minimum(jnp.maximum(drawn, -most), most).astype(dtype)


def setup_inputs(seed: int = 0, part: int = 0) -> dict:
    streams_of = jax.random.split(jax.random.key(seed), 3)
    own_keys = jax.random.split(jax.random.fold_in(streams_of[2], part), 3)
    return {
        "slab": bell_draw(own_keys[0], (NX, NS, CELLS), 1.0, 6.0, ((0, 16),)),
        "factor": bell_draw(own_keys[1], (NX, RANK), NX ** -0.5, 0.125, ((0, 16),)),
    }


def reference(slab, factor):
    unfolded = slab.reshape(NX, NS * CELLS)
    gram = lax.dot_general(unfolded, unfolded, (((1,), (1,)), ((), ())), preferred_element_type=jnp.float32)
    gram = gram / jnp.float32(NS * CELLS)
    core = lax.dot_general(unfolded, factor, (((0,), (0,)), ((), ())), preferred_element_type=jnp.float32)
    return gram, core
```

```python
import jax
import jax.numpy as jnp
import numpy as np
from jax import lax
from jax.sharding import Mesh
from jax.sharding import PartitionSpec as P

AXES = ("groups", "z", "y", "c")
CHUNKS = 4


def nt_dot(a, b):
    return lax.dot_general(a, b, (((1,), (1,)), ((), ())), preferred_element_type=jnp.float32)


def on_device(planes, slab, factor):
    rows, species, cells = slab.shape
    total = species * cells
    z, y, c = (lax.axis_index(name) for name in ("z", "y", "c"))
    width = total // (planes * CHUNKS)
    full_factor = lax.all_gather(factor, ("z", "y", "c"), axis=0, tiled=True)
    sent = [slab.reshape(rows, planes, CHUNKS, width)[:, :, j].transpose(1, 0, 2) for j in range(CHUNKS)]
    swap = [(0, 1), (1, 0)]
    sums = [jnp.float32(0)] * 4
    core = jnp.zeros((width, factor.shape[1]), jnp.float32)
    for j in range(CHUNKS):
        stack = sent[j]
        for shift in range(1, planes):
            piece = lax.dynamic_index_in_dim(sent[j], (z + shift) % planes, 0, keepdims=True)
            came = lax.ppermute(piece, "z", [(i, (i + shift) % planes) for i in range(planes)])
            stack = lax.dynamic_update_slice(stack, came, ((z - shift) % planes, 0, 0))
        across = lax.ppermute(stack, "y", swap)
        blocks = [stack, lax.ppermute(stack, "c", swap), across, lax.ppermute(across, "c", swap)]
        flat = [b.reshape(planes * rows, width) for b in blocks]
        for k in range(4):
            sums[k] = sums[k] + nt_dot(flat[0], flat[k])
        mine = y * 2 + c == j
        factors = full_factor.reshape(planes, 2, 2, rows, -1)
        part = jnp.float32(0)
        for k in range(4):
            f = lax.dynamic_index_in_dim(factors, y ^ (k // 2), 1, keepdims=False)
            f = lax.dynamic_index_in_dim(f, c ^ (k % 2), 1, keepdims=False)
            part = part + lax.dot_general(
                flat[k], f.reshape(planes * rows, -1), (((0,), (0,)), ((), ())), preferred_element_type=jnp.float32
            )
        core = jnp.where(mine, part, core)
    gram = jnp.concatenate(sums, axis=1)
    gram = lax.psum_scatter(gram, "z", scatter_dimension=0, tiled=True)
    gram = gram.reshape(rows, 2, 2, planes, rows)
    gram = jnp.where(y == 1, gram[:, ::-1], gram)
    gram = jnp.where(c == 1, gram[:, :, ::-1], gram)
    gram = gram.transpose(0, 3, 1, 2, 4).reshape(rows, -1) / jnp.float32(total)
    return (gram, core)


def solution(mesh):
    groups, n = mesh.devices.shape
    planes = n // 4
    fine = Mesh(np.reshape(mesh.devices, (groups, planes, 2, 2)), AXES)
    spec = P(AXES)
    return jax.shard_map(
        lambda slab, factor: on_device(planes, slab, factor),
        mesh=fine,
        in_specs=(spec, spec),
        out_specs=(spec, spec),
        check_vma=False,
    )
```

```python
import functools

import jax
import jax.numpy as jnp
import numpy as np
from jax import lax
from jax.experimental import pallas as pl
from jax.experimental.pallas import tpu as pltpu
from jax.sharding import Mesh
from jax.sharding import PartitionSpec as P

AXES = ("groups", "z", "y", "c")
BLOCK = 16
LANES = 128


def nt_dot(a, b):
    return lax.dot_general(a, b, (((1,), (1,)), ((), ())), preferred_element_type=jnp.float32)


def tn_dot(a, b):
    return lax.dot_general(a, b, (((0,), (0,)), ((), ())), preferred_element_type=jnp.float32)


def unfold_kernel(planes, per_plane, group, start, extra, z_ref, *refs):
    ins, outs, wide = refs[:planes], refs[planes + extra : -1], refs[-1]
    rows = ins[0].shape[0]
    for shift in range(planes):
        first = lax.rem(lax.rem(z_ref[0] + shift, planes) * per_plane + start, BLOCK)
        wide[...] = ins[shift][...].astype(jnp.float32).reshape(rows * BLOCK, LANES)
        for s in range(group):
            taken = wide[pl.ds(first + s, rows, stride=BLOCK), :]
            outs[shift][:, s * LANES : (s + 1) * LANES] = taken.astype(jnp.bfloat16)
        if extra:
            outs[shift][:, group * LANES :] = refs[planes][...]


def unfold(slab, factor, z, planes, group, start, lane_block):
    rows, species, cells = slab.shape
    per_plane = species // planes
    step = min(rows, 32)
    rank = factor.shape[1] if factor is not None else 0
    width = group * LANES + rank
    in_specs = [
        pl.BlockSpec(
            (step, BLOCK, LANES),
            lambda i, z_ref, shift=shift: (
                i, lax.div(lax.rem(z_ref[0] + shift, planes) * per_plane + start, BLOCK), lane_block
            ),
        )
        for shift in range(planes)
    ]
    operands = [slab] * planes
    if rank:
        in_specs.append(pl.BlockSpec((step, rank), lambda i, z_ref: (i, 0)))
        operands.append(factor)
    return pl.pallas_call(
        functools.partial(unfold_kernel, planes, per_plane, group, start, 1 if rank else 0),
        out_shape=[jax.ShapeDtypeStruct((rows, width), slab.dtype)] * planes,
        grid_spec=pltpu.PrefetchScalarGridSpec(
            num_scalar_prefetch=1,
            grid=(rows // step,),
            in_specs=in_specs,
            out_specs=[pl.BlockSpec((step, width), lambda i, z_ref: (i, 0))] * planes,
            scratch_shapes=[pltpu.VMEM((step * BLOCK, LANES), jnp.float32)],
        ),
        compiler_params=pltpu.CompilerParams(vmem_limit_bytes=16 * 2**20),
        cost_estimate=pl.CostEstimate(
            flops=0, bytes_accessed=planes * rows * (BLOCK * LANES + width) * 2, transcendentals=0
        ),
        name="unfold",
    )(z.reshape(1).astype(jnp.int32), *operands)


def on_device(planes, slab, factor):
    rows, species, cells = slab.shape
    rank = factor.shape[1]
    total = species * cells
    z, y, c = (lax.axis_index(name) for name in ("z", "y", "c"))
    per_plane = species // planes
    group = min(per_plane, 8)
    halves = cells // LANES
    chunks = [(o, h) for o in range(per_plane // group) for h in range(halves)]
    swap = [(0, 1), (1, 0)]
    sums = [jnp.float32(0)] * 4
    held, earlier = [], None
    width = group * LANES
    factors = None
    for j, (o, h) in enumerate(chunks):
        pieces = unfold(slab, factor if j == 1 else None, z, planes, group, o * group, h)
        came = []
        for shift in range(1, planes):
            piece = pieces[shift]
            if j:
                piece, _ = lax.optimization_barrier((piece, earlier[shift - 1]))
            came.append(lax.ppermute(piece, "z", [(i, (i + shift) % planes) for i in range(planes)]))
        earlier = came
        stack = jnp.zeros((planes,) + pieces[0].shape, slab.dtype)
        for shift in range(planes):
            piece = came[shift - 1] if shift else pieces[0]
            stack = lax.dynamic_update_slice(stack, piece[None], ((z - shift) % planes, 0, 0))
        across = lax.ppermute(stack, "y", swap)
        blocks = [stack, lax.ppermute(stack, "c", swap), across, lax.ppermute(across, "c", swap)]
        flat = [b.reshape(planes * rows, -1) for b in blocks]
        if j == 1:
            factors = [b[:, width:] for b in flat]
            flat = [b[:, :width] for b in flat]
        for k in range(4):
            sums[k] = sums[k] + nt_dot(flat[0], flat[k])
        held.append(flat)
    own = per_plane // 4
    at = (y * 2 + c) * own
    parts = []
    for h in range(halves):
        part = jnp.float32(0)
        for k in range(4):
            taken = None
            for j, (o, half) in enumerate(chunks):
                if half == h:
                    piece = lax.dynamic_slice_in_dim(held[j][k], (at % group) * LANES, own * LANES, 1)
                    taken = piece if taken is None else jnp.where(at // group == o, piece, taken)
            part = part + tn_dot(taken, factors[k])
        parts.append(part.reshape(own, 1, LANES, rank))
    core = jnp.concatenate(parts, axis=1).reshape(own * cells, rank)
    gram = jnp.concatenate(sums, axis=1)
    gram = lax.psum_scatter(gram, "z", scatter_dimension=0, tiled=True)
    gram = gram.reshape(rows, 2, 2, planes, rows)
    gram = jnp.where(y == 1, gram[:, ::-1], gram)
    gram = jnp.where(c == 1, gram[:, :, ::-1], gram)
    gram = gram.transpose(0, 3, 1, 2, 4).reshape(rows, -1) / jnp.float32(total)
    return (gram, core)


def solution(mesh):
    groups, n = mesh.devices.shape
    planes = n // 4
    fine = Mesh(np.reshape(mesh.devices, (groups, planes, 2, 2)), AXES)
    spec = P(AXES)
    return jax.shard_map(
        lambda slab, factor: on_device(planes, slab, factor),
        mesh=fine,
        in_specs=(spec, spec),
        out_specs=(spec, spec),
        check_vma=False,
    )
```

```python
import functools

import jax
import jax.numpy as jnp
import numpy as np
from jax import lax
from jax.experimental import pallas as pl
from jax.experimental.pallas import tpu as pltpu
from jax.sharding import Mesh
from jax.sharding import PartitionSpec as P

AXES = ("groups", "z", "y", "c")
BLOCK = 16
LANES = 128
DEPTH = 512
SWAP = [(0, 1), (1, 0)]


def parts_of(rows):
    sizes = [rows // 4] * 3 + [rows // 8] * 2 if rows >= 8 * BLOCK else [BLOCK] * (rows // BLOCK)
    return [(sum(sizes[:i]), size) for i, size in enumerate(sizes)]


def nt_dot(a, b):
    return lax.dot_general(a, b, (((1,), (1,)), ((), ())), preferred_element_type=jnp.float32)


def tn_dot(a, b):
    return lax.dot_general(a, b, (((0,), (0,)), ((), ())), preferred_element_type=jnp.float32)


def unfold_kernel(planes, per_plane, z_ref, *refs):
    ins, factor, outs, wide = refs[:planes], refs[planes], refs[planes + 1 : -1], refs[-1]
    rows, _, cells = ins[0].shape
    for shift in range(planes):
        first = lax.rem(lax.rem(z_ref[0] + shift, planes) * per_plane, BLOCK)
        for h in range(0, cells, LANES):
            wide[...] = ins[shift][:, :, h : h + LANES].astype(jnp.float32).reshape(rows * BLOCK, LANES)
            for s in range(per_plane):
                at = s * cells + h
                outs[shift][:, at : at + LANES] = wide[pl.ds(first + s, rows, stride=BLOCK), :].astype(jnp.bfloat16)
        outs[shift][:, per_plane * cells :] = factor[...]


def unfold(slab, factor, z, planes, start, size):
    _, species, cells = slab.shape
    rank = factor.shape[1]
    per_plane = species // planes
    width = per_plane * cells + rank
    first = start // BLOCK
    in_specs = [
        pl.BlockSpec(
            (BLOCK, BLOCK, cells),
            lambda i, z_ref, shift=shift: (
                i + first, lax.div(lax.rem(z_ref[0] + shift, planes) * per_plane, BLOCK), 0
            ),
        )
        for shift in range(planes)
    ]
    in_specs.append(pl.BlockSpec((BLOCK, rank), lambda i, z_ref: (i + first, 0)))
    return pl.pallas_call(
        functools.partial(unfold_kernel, planes, per_plane),
        out_shape=[jax.ShapeDtypeStruct((size, width), slab.dtype)] * planes,
        grid_spec=pltpu.PrefetchScalarGridSpec(
            num_scalar_prefetch=1,
            grid=(size // BLOCK,),
            in_specs=in_specs,
            out_specs=[pl.BlockSpec((BLOCK, width), lambda i, z_ref: (i, 0))] * planes,
            scratch_shapes=[pltpu.VMEM((BLOCK * BLOCK, LANES), jnp.float32)],
        ),
        compiler_params=pltpu.CompilerParams(vmem_limit_bytes=16 * 2**20),
        cost_estimate=pl.CostEstimate(
            flops=0, bytes_accessed=planes * size * (BLOCK * cells + width) * 2, transcendentals=0
        ),
        name="unfold",
    )(z.reshape(1).astype(jnp.int32), *([slab] * planes), factor)


def products_kernel(planes, sizes, *refs):
    last = len(sizes) - 1
    size = sizes[last]
    blocks = [[refs[4 * j + k][...] for k in range(4)] for j in range(last + 1)]
    out = refs[-1]
    first = pl.program_id(0) == 0

    @pl.when(first)
    def _():
        out[...] = jnp.zeros_like(out)

    every = jnp.concatenate([b for part in blocks for b in part], axis=0)
    step = 4 * planes * size
    for n in range(every.shape[0] // step):
        got = nt_dot(blocks[last][0], every[n * step : (n + 1) * step])
        out[:, n * size : (n + 1) * size, :] += got.reshape(planes, size, step)
    start = sum(sizes)
    new = every[every.shape[0] - step :]
    for j in range(last):
        got = nt_dot(blocks[j][0], new)
        out[:, start : start + sizes[j], :] += got.reshape(planes, sizes[j], step)
        start += sizes[j]


def products(planes, sizes, blocks, depth):
    total = sum(sizes)
    shape = (planes, 2 * total - sizes[-1], 4 * planes * sizes[-1])
    tile = min(depth, DEPTH)
    return pl.pallas_call(
        functools.partial(products_kernel, planes, sizes),
        out_shape=jax.ShapeDtypeStruct(shape, jnp.float32),
        grid=(depth // tile,),
        in_specs=[pl.BlockSpec((b.shape[0], tile), lambda i: (0, i)) for part in blocks for b in part],
        out_specs=pl.BlockSpec(shape, lambda i: (0, 0, 0)),
        compiler_params=pltpu.CompilerParams(vmem_limit_bytes=40 * 2**20),
        cost_estimate=pl.CostEstimate(
            flops=2 * shape[0] * shape[1] * shape[2] * depth,
            bytes_accessed=4 * planes * total * depth * 2 + 4 * shape[0] * shape[1] * shape[2],
            transcendentals=0,
        ),
        name="products",
    )(*[b for part in blocks for b in part])


def order_kernel(planes, parts, scale, place_ref, *refs):
    sums, out = refs[:-1], refs[-1]
    rows = out.shape[0]

    def block(i, j, k, z):
        (start_i, size_i), (start_j, size_j) = parts[i], parts[j]
        if j <= i:
            step = 4 * planes * size_i
            at = 4 * planes * start_j + (k * planes + z) * size_j
            n, lane = at // step, at % step
            return sums[i][n * size_i : (n + 1) * size_i, lane : lane + size_j]
        start = start_j + size_j + start_i
        lane = (k * planes + z) * size_j
        return sums[j][start : start + size_i, lane : lane + size_j]

    for place in range(4):

        @pl.when(place_ref[0] == place)
        def _():
            for i, (start, size) in enumerate(parts):
                for at in range(0, 4 * planes * rows, LANES):
                    pieces = []
                    for column in range(at // rows, (at + LANES - 1) // rows + 1):
                        z, other = column // 4, column % 4
                        for j in range(len(parts)):
                            pieces.append(block(i, j, place ^ other, z))
                    taken = jnp.concatenate(pieces, axis=1)
                    out[start : start + size, at : at + LANES] = taken * scale


def order(planes, parts, total, place, sums):
    rows = parts[-1][0] + parts[-1][1]
    return pl.pallas_call(
        functools.partial(order_kernel, planes, parts, 1.0 / total),
        out_shape=jax.ShapeDtypeStruct((rows, 4 * planes * rows), jnp.float32),
        in_specs=[pl.BlockSpec(memory_space=pltpu.SMEM)] + [pl.BlockSpec(memory_space=pltpu.VMEM)] * len(sums),
        out_specs=pl.BlockSpec(memory_space=pltpu.VMEM),
        compiler_params=pltpu.CompilerParams(vmem_limit_bytes=16 * 2**20),
        name="order",
    )(place.reshape(1).astype(jnp.int32), *sums)


def after(value, *others):
    return lax.optimization_barrier((value, others))[0]


def on_device(planes, slab, factor):
    rows, species, cells = slab.shape
    rank = factor.shape[1]
    total = species * cells
    depth = total // planes
    z, y, c = (lax.axis_index(name) for name in ("z", "y", "c"))
    parts = parts_of(rows)
    came, waits, held, made, sums = [], [], [], [], []
    for i, (start, size) in enumerate(parts):
        pieces = unfold(slab, factor, z, planes, start, size)
        arrived = []
        for shift in range(1, planes):
            piece = pieces[shift]
            if i:
                piece = after(piece, came[i - 1][shift - 1], *(waits[i - 2] if i > 1 else ()), *made[: max(i - 2, 0)])
            arrived.append(lax.ppermute(piece, "z", [(s, (s + shift) % planes) for s in range(planes)]))
        came.append(arrived)
        stack = jnp.zeros((planes,) + pieces[0].shape, slab.dtype)
        for shift in range(planes):
            piece = arrived[shift - 1] if shift else pieces[0]
            stack = lax.dynamic_update_slice(stack, piece[None], ((z - shift) % planes, 0, 0))
        stack = stack.reshape(planes * size, -1)
        across = lax.ppermute(stack, "y", SWAP)
        beside = lax.ppermute(stack, "c", SWAP)
        waits.append((across, beside))
        held.append([stack, beside, across, lax.ppermute(across, "c", SWAP)])
        part = products(planes, [size for _, size in parts[: i + 1]], held, depth)
        if i:
            part = after(part, made[-1])
        made.append(part)
        sums.append(lax.psum_scatter(part, "z", scatter_dimension=0, tiled=False))
    gram = order(planes, parts, total, y * 2 + c, sums)
    own = depth // 4
    core = jnp.float32(0)
    for part in held:
        for b in part:
            b = after(b, made[-1])
            taken = lax.dynamic_slice_in_dim(b[:, :depth], (y * 2 + c) * own, own, 1)
            core = core + tn_dot(taken, b[:, depth:])
    return (gram, core)


def solution(mesh):
    groups, n = mesh.devices.shape
    planes = n // 4
    fine = Mesh(np.reshape(mesh.devices, (groups, planes, 2, 2)), AXES)
    spec = P(AXES)
    return jax.shard_map(
        lambda slab, factor: on_device(planes, slab, factor),
        mesh=fine,
        in_specs=(spec, spec),
        out_specs=(spec, spec),
        check_vma=False,
    )
```

```python
import functools

import jax
import jax.numpy as jnp
import numpy as np
from jax import lax
from jax.experimental import pallas as pl
from jax.experimental.pallas import tpu as pltpu
from jax.sharding import Mesh
from jax.sharding import PartitionSpec as P

AXES = ("groups", "z", "y", "c")
BLOCK = 16
LANES = 128
SWAP = [(0, 1), (1, 0)]


def chunks_of(per_plane):
    unit = per_plane // 4
    sizes = [unit] * 3 + ([unit // 2] * 2 if unit % 2 == 0 else [unit])
    return [(sum(sizes[:i]), size) for i, size in enumerate(sizes)]


def nt_dot(a, b):
    return lax.dot_general(a, b, (((1,), (1,)), ((), ())), preferred_element_type=jnp.float32)


def tn_dot(a, b):
    return lax.dot_general(a, b, (((0,), (0,)), ((), ())), preferred_element_type=jnp.float32)


def after(value, *others):
    return lax.optimization_barrier((value, others))[0]


def unfold_kernel(planes, per_plane, chunks, extra, z_ref, *refs):
    ins, factor, outs, wide = refs[:planes], refs[planes], refs[planes + 1 : -1], refs[-1]
    rows, _, cells = ins[0].shape
    for shift in range(planes):
        first = lax.rem(lax.rem(z_ref[0] + shift, planes) * per_plane, BLOCK)
        for h in range(0, cells, LANES):
            wide[...] = ins[shift][:, :, h : h + LANES].astype(jnp.float32).reshape(rows * BLOCK, LANES)
            for n, (start, size) in enumerate(chunks):
                out = outs[n * planes + shift]
                for s in range(size):
                    taken = wide[pl.ds(first + start + s, rows, stride=BLOCK), :]
                    out[:, s * cells + h : s * cells + h + LANES] = taken.astype(jnp.bfloat16)
        if extra is not None:
            outs[extra * planes + shift][:, chunks[extra][1] * cells :] = factor[...]


def unfold(slab, factor, z, planes, chunks, extra):
    rows, species, cells = slab.shape
    rank = factor.shape[1]
    per_plane = species // planes
    step = min(rows, 32)
    widths = [size * cells + (rank if n == extra else 0) for n, (_, size) in enumerate(chunks)]
    in_specs = [
        pl.BlockSpec(
            (step, BLOCK, cells),
            lambda i, z_ref, shift=shift: (i, lax.div(lax.rem(z_ref[0] + shift, planes) * per_plane, BLOCK), 0),
        )
        for shift in range(planes)
    ]
    in_specs.append(pl.BlockSpec((step, rank), lambda i, z_ref: (i, 0)))
    out = pl.pallas_call(
        functools.partial(unfold_kernel, planes, per_plane, chunks, extra),
        out_shape=[jax.ShapeDtypeStruct((rows, width), slab.dtype) for width in widths for _ in range(planes)],
        grid_spec=pltpu.PrefetchScalarGridSpec(
            num_scalar_prefetch=1,
            grid=(rows // step,),
            in_specs=in_specs,
            out_specs=[pl.BlockSpec((step, width), lambda i, z_ref: (i, 0)) for width in widths for _ in range(planes)],
            scratch_shapes=[pltpu.VMEM((step * BLOCK, LANES), jnp.float32)],
        ),
        compiler_params=pltpu.CompilerParams(vmem_limit_bytes=24 * 2**20),
        cost_estimate=pl.CostEstimate(
            flops=0, bytes_accessed=planes * rows * (BLOCK * cells + sum(widths)) * 2, transcendentals=0
        ),
        name="unfold",
    )(z.reshape(1).astype(jnp.int32), *([slab] * planes), factor)
    return [out[n * planes : (n + 1) * planes] for n in range(len(chunks))]


def finish_kernel(planes, scale, place_ref, *refs):
    out = refs[-1]
    rows = out.shape[0]
    sums = []
    for pair in range(2):
        own, below, above = refs[3 * pair : 3 * pair + 3]
        sums.append((own[...] + below[...] + above[...]) * scale)

    def block(k, z):
        at = ((k % 2) * planes + z) * rows
        return sums[k // 2][:, at : at + rows]

    for place in range(4):

        @pl.when(place_ref[0] == place)
        def _():
            for z in range(planes):
                pieces = [block(place ^ other, z) for other in range(4)]
                out[:, z * 4 * rows : (z + 1) * 4 * rows] = jnp.concatenate(pieces, axis=1)


def finish(planes, total, place, parts):
    rows = parts[0].shape[0]
    return pl.pallas_call(
        functools.partial(finish_kernel, planes, 1.0 / total),
        out_shape=jax.ShapeDtypeStruct((rows, 4 * planes * rows), jnp.float32),
        in_specs=[pl.BlockSpec(memory_space=pltpu.SMEM)] + [pl.BlockSpec(memory_space=pltpu.VMEM)] * len(parts),
        out_specs=pl.BlockSpec(memory_space=pltpu.VMEM),
        compiler_params=pltpu.CompilerParams(vmem_limit_bytes=24 * 2**20),
        name="finish",
    )(place.reshape(1).astype(jnp.int32), *parts)


def chain(planes, z, sums, up):
    rows = sums.shape[0] // planes
    got = None
    for step in range(1, planes):
        plane = planes - step + z if up else z - planes + step
        sent = lax.dynamic_slice_in_dim(sums, jnp.clip(plane, 0, planes - 1) * rows, rows, 0)
        if got is not None:
            sent = sent + got
        pairs = [(i, i + 1) for i in range(step)] if up else [(planes - 1 - i, planes - 2 - i) for i in range(step)]
        got = lax.ppermute(sent, "z", pairs)
    return got


def on_device(planes, slab, factor):
    rows, species, cells = slab.shape
    rank = factor.shape[1]
    total = species * cells
    z, y, c = (lax.axis_index(name) for name in ("z", "y", "c"))
    place = y * 2 + c
    per_plane = species // planes
    chunks = chunks_of(per_plane)
    last = len(chunks) - 1
    pieces = unfold(slab, factor, z, planes, chunks[:1], None) + unfold(slab, factor, z, planes, chunks[1:], 0)

    def stacked(parts):
        stack = jnp.zeros((planes,) + parts[0].shape, slab.dtype)
        for shift in range(planes):
            stack = lax.dynamic_update_slice(stack, parts[shift][None], ((z - shift) % planes, 0, 0))
        return stack.reshape(planes * rows, -1)

    came, waits, held = [], [], []
    for j in range(last + 1):
        arrived = [pieces[j][0]]
        for shift in range(1, planes):
            piece = pieces[j][shift]
            if j:
                piece = after(piece, came[j - 1][shift], *(waits[j - 2] if j > 1 else ()))
            arrived.append(lax.ppermute(piece, "z", [(s, (s + shift) % planes) for s in range(planes)]))
        came.append(arrived)
        stack = stacked(arrived)
        across = lax.ppermute(stack, "y", SWAP)
        beside = lax.ppermute(stack, "c", SWAP)
        waits.append((across, beside))
        held.append([stack, beside, across, lax.ppermute(across, "c", SWAP)])
    flat = [[b[:, : size * cells] for b in held[j]] for j, (_, size) in enumerate(chunks)]
    factors = [b[:, chunks[1][1] * cells :] for b in held[1]]
    sums = [sum(nt_dot(flat[j][0], flat[j][k]) for j in range(last + 1)) for k in range(4)]
    parts = []
    for pair in range(2):
        both = jnp.concatenate(sums[2 * pair : 2 * pair + 2], axis=1)
        parts.append(lax.dynamic_slice_in_dim(both, z * rows, rows, 0))
        parts.append(chain(planes, z, both, True))
        parts.append(chain(planes, z, both, False))
    gram = finish(planes, total, place, parts)
    own = per_plane // 4
    whole = [sum(tn_dot(flat[j][k], factors[k]) for k in range(4)) for j in range(last + 1)]
    whole = jnp.concatenate(whole, axis=0)
    core = lax.dynamic_slice_in_dim(whole, place * own * cells, own * cells, 0)
    return (gram, core)


def solution(mesh):
    groups, n = mesh.devices.shape
    planes = n // 4
    fine = Mesh(np.reshape(mesh.devices, (groups, planes, 2, 2)), AXES)
    spec = P(AXES)
    return jax.shard_map(
        lambda slab, factor: on_device(planes, slab, factor),
        mesh=fine,
        in_specs=(spec, spec),
        out_specs=(spec, spec),
        check_vma=False,
    )
```

```python
import functools

import jax
import jax.numpy as jnp
import numpy as np
from jax import lax
from jax.experimental import pallas as pl
from jax.experimental.pallas import tpu as pltpu
from jax.sharding import Mesh
from jax.sharding import PartitionSpec as P

AXES = ("groups", "z", "y", "c")
BLOCK = 16
LANES = 128
SWAP = [(0, 1), (1, 0)]


def chunks_of(per_plane):
    unit = per_plane // 4
    sizes = [unit] * 3 + ([unit // 2] * 2 if unit % 2 == 0 else [unit])
    return [(sum(sizes[:i]), size) for i, size in enumerate(sizes)]


def nt_dot(a, b):
    return lax.dot_general(a, b, (((1,), (1,)), ((), ())), preferred_element_type=jnp.float32)


def tn_dot(a, b):
    return lax.dot_general(a, b, (((0,), (0,)), ((), ())), preferred_element_type=jnp.float32)


def after(value, *others):
    return lax.optimization_barrier((value, others))[0]


def unfold_kernel(planes, per_plane, chunks, extra, z_ref, *refs):
    ins, factor, outs, wide = refs[:planes], refs[planes], refs[planes + 1 : -1], refs[-1]
    rows, _, cells = ins[0].shape
    for shift in range(planes):
        first = lax.rem((z_ref[0] ^ shift) * per_plane, BLOCK)
        for h in range(0, cells, LANES):
            wide[...] = ins[shift][:, :, h : h + LANES].astype(jnp.float32).reshape(rows * BLOCK, LANES)
            for n, (start, size) in enumerate(chunks):
                out = outs[n * planes + shift]
                for s in range(size):
                    taken = wide[pl.ds(first + start + s, rows, stride=BLOCK), :]
                    out[:, s * cells + h : s * cells + h + LANES] = taken.astype(jnp.bfloat16)
        if extra is not None:
            outs[extra * planes + shift][:, chunks[extra][1] * cells :] = factor[...]


def unfold(slab, factor, z, planes, chunks, extra):
    rows, species, cells = slab.shape
    rank = factor.shape[1]
    per_plane = species // planes
    step = min(rows, 32)
    widths = [size * cells + (rank if n == extra else 0) for n, (_, size) in enumerate(chunks)]
    in_specs = [
        pl.BlockSpec(
            (step, BLOCK, cells),
            lambda i, z_ref, shift=shift: (i, lax.div((z_ref[0] ^ shift) * per_plane, BLOCK), 0),
        )
        for shift in range(planes)
    ]
    in_specs.append(pl.BlockSpec((step, rank), lambda i, z_ref: (i, 0)))
    out = pl.pallas_call(
        functools.partial(unfold_kernel, planes, per_plane, chunks, extra),
        out_shape=[jax.ShapeDtypeStruct((rows, width), slab.dtype) for width in widths for _ in range(planes)],
        grid_spec=pltpu.PrefetchScalarGridSpec(
            num_scalar_prefetch=1,
            grid=(rows // step,),
            in_specs=in_specs,
            out_specs=[pl.BlockSpec((step, width), lambda i, z_ref: (i, 0)) for width in widths for _ in range(planes)],
            scratch_shapes=[pltpu.VMEM((step * BLOCK, LANES), jnp.float32)],
        ),
        compiler_params=pltpu.CompilerParams(vmem_limit_bytes=24 * 2**20),
        cost_estimate=pl.CostEstimate(
            flops=0, bytes_accessed=planes * rows * (BLOCK * cells + sum(widths)) * 2, transcendentals=0
        ),
        name="unfold",
    )(z.reshape(1).astype(jnp.int32), *([slab] * planes), factor)
    return [out[n * planes : (n + 1) * planes] for n in range(len(chunks))]


def finish_kernel(planes, scale, place_ref, *refs):
    out = refs[-1]
    rows = out.shape[0]
    sums = []
    for pair in range(2):
        own, below, above = refs[3 * pair : 3 * pair + 3]
        sums.append((own[...] + below[...] + above[...]) * scale)

    def block(k, z):
        at = ((k % 2) * planes + z) * rows
        return sums[k // 2][:, at : at + rows]

    for place in range(4):

        @pl.when(place_ref[0] == place)
        def _():
            for z in range(planes):
                pieces = [block(place ^ other, z) for other in range(4)]
                out[:, z * 4 * rows : (z + 1) * 4 * rows] = jnp.concatenate(pieces, axis=1)


def finish(planes, total, place, parts):
    rows = parts[0].shape[0]
    return pl.pallas_call(
        functools.partial(finish_kernel, planes, 1.0 / total),
        out_shape=jax.ShapeDtypeStruct((rows, 4 * planes * rows), jnp.float32),
        in_specs=[pl.BlockSpec(memory_space=pltpu.SMEM)] + [pl.BlockSpec(memory_space=pltpu.VMEM)] * len(parts),
        out_specs=pl.BlockSpec(memory_space=pltpu.VMEM),
        compiler_params=pltpu.CompilerParams(vmem_limit_bytes=24 * 2**20),
        name="finish",
    )(place.reshape(1).astype(jnp.int32), *parts)


def chain(planes, z, sums, up):
    rows = sums.shape[0] // planes
    got = None
    for step in range(1, planes):
        plane = planes - step + z if up else z - planes + step
        sent = lax.dynamic_slice_in_dim(sums, jnp.clip(plane, 0, planes - 1) * rows, rows, 0)
        if got is not None:
            sent = sent + got
        pairs = [(i, i + 1) for i in range(step)] if up else [(planes - 1 - i, planes - 2 - i) for i in range(step)]
        got = lax.ppermute(sent, "z", pairs)
    return got


def on_device(planes, slab, factor):
    rows, species, cells = slab.shape
    rank = factor.shape[1]
    total = species * cells
    z, y, c = (lax.axis_index(name) for name in ("z", "y", "c"))
    place = y * 2 + c
    per_plane = species // planes
    chunks = chunks_of(per_plane)
    last = len(chunks) - 1
    pieces = unfold(slab, factor, z, planes, chunks[:1], None) + unfold(slab, factor, z, planes, chunks[1:], 0)

    def stacked(parts):
        stack = jnp.zeros((planes,) + parts[0].shape, slab.dtype)
        for shift in range(planes):
            stack = lax.dynamic_update_slice(stack, parts[shift][None], (z ^ shift, 0, 0))
        return stack.reshape(planes * rows, -1)

    came, held = [], []
    across = pair = None
    for j in range(last + 1):
        arrived = [pieces[j][0]]
        for shift in range(1, planes):
            piece = pieces[j][shift]
            if j:
                piece = after(piece, came[j - 1][shift], *([held[j - 2][2]] if j > 1 and shift == 1 else []))
            arrived.append(lax.ppermute(piece, "z", [(s, s ^ shift) for s in range(planes)]))
        came.append(arrived)
        stack = stacked(arrived)
        across = lax.ppermute(stack if across is None else after(stack, across), "y", SWAP)
        beside = lax.ppermute(stack if pair is None else after(stack, pair), "c", SWAP)
        pair = lax.ppermute(after(across, beside), "c", SWAP)
        held.append([stack, beside, across, pair])
    flat = [[b[:, : size * cells] for b in held[j]] for j, (_, size) in enumerate(chunks)]
    factors = [b[:, chunks[1][1] * cells :] for b in held[1]]
    sums = [sum(nt_dot(flat[j][0], flat[j][k]) for j in range(last + 1)) for k in range(4)]
    parts = []
    for pair in range(2):
        both = jnp.concatenate(sums[2 * pair : 2 * pair + 2], axis=1)
        parts.append(lax.dynamic_slice_in_dim(both, z * rows, rows, 0))
        parts.append(chain(planes, z, both, True))
        parts.append(chain(planes, z, both, False))
    gram = finish(planes, total, place, parts)
    own = per_plane // 4
    whole = [sum(tn_dot(flat[j][k], factors[k]) for k in range(4)) for j in range(last + 1)]
    whole = jnp.concatenate(whole, axis=0)
    core = lax.dynamic_slice_in_dim(whole, place * own * cells, own * cells, 0)
    return (gram, core)


def solution(mesh):
    groups, n = mesh.devices.shape
    planes = n // 4
    fine = Mesh(np.reshape(mesh.devices, (groups, planes, 2, 2)), AXES)
    spec = P(AXES)
    return jax.shard_map(
        lambda slab, factor: on_device(planes, slab, factor),
        mesh=fine,
        in_specs=(spec, spec),
        out_specs=(spec, spec),
        check_vma=False,
    )
```

```python
import functools

import jax
import jax.numpy as jnp
import numpy as np
from jax import lax
from jax.experimental import pallas as pl
from jax.experimental.pallas import tpu as pltpu
from jax.sharding import Mesh
from jax.sharding import PartitionSpec as P

AXES = ("groups", "z", "y", "c")
BLOCK = 16
LANES = 128
WINDOW = 4
SWAP = [(0, 1), (1, 0)]


def chunks_of(per_plane):
    unit = per_plane // 16
    sizes = [5 * unit, 5 * unit, 4 * unit, 2 * unit] if unit else [1] * per_plane
    return [(sum(sizes[:i]), size) for i, size in enumerate(sizes)]


def nt_dot(a, b):
    return lax.dot_general(a, b, (((1,), (1,)), ((), ())), preferred_element_type=jnp.float32)


def tn_dot(a, b):
    return lax.dot_general(a, b, (((0,), (0,)), ((), ())), preferred_element_type=jnp.float32)


def after(value, *others):
    return lax.optimization_barrier((value, others))[0]


def unfold_kernel(planes, per_plane, chunks, extra, z_ref, *refs):
    ins, factor, outs, wide = refs[:planes], refs[planes], refs[planes + 1 : -1], refs[-1]
    rows, _, cells = ins[0].shape
    for shift in range(planes):
        first = lax.rem(lax.rem(z_ref[0] + shift, planes) * per_plane, BLOCK)
        for h in range(0, cells, LANES):
            wide[...] = ins[shift][:, :, h : h + LANES].astype(jnp.float32).reshape(rows * BLOCK, LANES)
            for n, (start, size) in enumerate(chunks):
                out = outs[n * planes + shift]
                for s in range(size):
                    taken = wide[pl.ds(first + start + s, rows, stride=BLOCK), :]
                    out[:, s * cells + h : s * cells + h + LANES] = taken.astype(jnp.bfloat16)
        if extra is not None:
            outs[extra * planes + shift][:, chunks[extra][1] * cells :] = factor[...]


def unfold(slab, factor, z, planes, chunks, extra):
    rows, species, cells = slab.shape
    rank = factor.shape[1]
    per_plane = species // planes
    step = min(rows, 32)
    widths = [size * cells + (rank if n == extra else 0) for n, (_, size) in enumerate(chunks)]
    in_specs = [
        pl.BlockSpec(
            (step, BLOCK, cells),
            lambda i, z_ref, shift=shift: (i, lax.div(lax.rem(z_ref[0] + shift, planes) * per_plane, BLOCK), 0),
        )
        for shift in range(planes)
    ]
    in_specs.append(pl.BlockSpec((step, rank), lambda i, z_ref: (i, 0)))
    out = pl.pallas_call(
        functools.partial(unfold_kernel, planes, per_plane, chunks, extra),
        out_shape=[jax.ShapeDtypeStruct((rows, width), slab.dtype) for width in widths for _ in range(planes)],
        grid_spec=pltpu.PrefetchScalarGridSpec(
            num_scalar_prefetch=1,
            grid=(rows // step,),
            in_specs=in_specs,
            out_specs=[pl.BlockSpec((step, width), lambda i, z_ref: (i, 0)) for width in widths for _ in range(planes)],
            scratch_shapes=[pltpu.VMEM((step * BLOCK, LANES), jnp.float32)],
        ),
        compiler_params=pltpu.CompilerParams(vmem_limit_bytes=24 * 2**20),
        cost_estimate=pl.CostEstimate(
            flops=0, bytes_accessed=planes * rows * (BLOCK * cells + sum(widths)) * 2, transcendentals=0
        ),
        name="unfold",
    )(z.reshape(1).astype(jnp.int32), *([slab] * planes), factor)
    return [out[n * planes : (n + 1) * planes] for n in range(len(chunks))]


def finish_kernel(planes, scale, place_ref, *refs):
    out = refs[-1]
    rows = out.shape[0]
    sums = []
    for pair in range(2):
        own, below, above = refs[3 * pair : 3 * pair + 3]
        sums.append((own[...] + below[...] + above[...]) * scale)

    def block(k, z):
        at = ((k % 2) * planes + z) * rows
        return sums[k // 2][:, at : at + rows]

    for place in range(4):

        @pl.when(place_ref[0] == place)
        def _():
            for z in range(planes):
                pieces = [block(place ^ other, z) for other in range(4)]
                out[:, z * 4 * rows : (z + 1) * 4 * rows] = jnp.concatenate(pieces, axis=1)


def finish(planes, total, place, parts):
    rows = parts[0].shape[0]
    return pl.pallas_call(
        functools.partial(finish_kernel, planes, 1.0 / total),
        out_shape=jax.ShapeDtypeStruct((rows, 4 * planes * rows), jnp.float32),
        in_specs=[pl.BlockSpec(memory_space=pltpu.SMEM)] + [pl.BlockSpec(memory_space=pltpu.VMEM)] * len(parts),
        out_specs=pl.BlockSpec(memory_space=pltpu.VMEM),
        compiler_params=pltpu.CompilerParams(vmem_limit_bytes=24 * 2**20),
        name="finish",
    )(place.reshape(1).astype(jnp.int32), *parts)


def chain(planes, z, sums, up):
    rows = sums.shape[0] // planes
    got = None
    for step in range(1, planes):
        plane = planes - step + z if up else z - planes + step
        sent = lax.dynamic_slice_in_dim(sums, jnp.clip(plane, 0, planes - 1) * rows, rows, 0)
        if got is not None:
            sent = sent + got
        pairs = [(i, i + 1) for i in range(step)] if up else [(planes - 1 - i, planes - 2 - i) for i in range(step)]
        got = lax.ppermute(sent, "z", pairs)
    return got


def on_device(planes, slab, factor):
    rows, species, cells = slab.shape
    rank = factor.shape[1]
    total = species * cells
    z, y, c = (lax.axis_index(name) for name in ("z", "y", "c"))
    place = y * 2 + c
    per_plane = species // planes
    chunks = chunks_of(per_plane)
    last = len(chunks) - 1
    pieces = unfold(slab, factor, z, planes, chunks[:1], None) + unfold(slab, factor, z, planes, chunks[1:], 0)

    def stacked(parts):
        stack = jnp.zeros((planes,) + parts[0].shape, slab.dtype)
        for shift in range(planes):
            stack = lax.dynamic_update_slice(stack, parts[shift][None], ((z - shift) % planes, 0, 0))
        return stack.reshape(planes * rows, -1)

    sent, waits, held = [], [], []
    for j in range(last + 1):
        arrived = [pieces[j][0]]
        for shift in range(1, planes):
            piece = pieces[j][shift]
            if len(sent) >= WINDOW:
                piece = after(piece, sent[-WINDOW], *(waits[min(j, last - 1) - 2] if j > 1 else ()))
            sent.append(lax.ppermute(piece, "z", [(s, (s + shift) % planes) for s in range(planes)]))
            arrived.append(sent[-1])
        stack = stacked(arrived)
        across = lax.ppermute(stack, "y", SWAP)
        beside = lax.ppermute(stack, "c", SWAP)
        waits.append((across, beside))
        held.append([stack, beside, across, lax.ppermute(across, "c", SWAP)])
    flat = [[b[:, : size * cells] for b in held[j]] for j, (_, size) in enumerate(chunks)]
    factors = [b[:, chunks[1][1] * cells :] for b in held[1]]
    sums = [sum(nt_dot(flat[j][0], flat[j][k]) for j in range(last + 1)) for k in range(4)]
    parts = []
    for pair in range(2):
        both = jnp.concatenate(sums[2 * pair : 2 * pair + 2], axis=1)
        parts.append(lax.dynamic_slice_in_dim(both, z * rows, rows, 0))
        parts.append(chain(planes, z, both, True))
        parts.append(chain(planes, z, both, False))
    gram = finish(planes, total, place, parts)
    own = per_plane // 4
    whole = [sum(tn_dot(flat[j][k], factors[k]) for k in range(4)) for j in range(last + 1)]
    whole = jnp.concatenate(whole, axis=0)
    core = lax.dynamic_slice_in_dim(whole, place * own * cells, own * cells, 0)
    return (gram, core)


def solution(mesh):
    groups, n = mesh.devices.shape
    planes = n // 4
    fine = Mesh(np.reshape(mesh.devices, (groups, planes, 2, 2)), AXES)
    spec = P(AXES)
    return jax.shard_map(
        lambda slab, factor: on_device(planes, slab, factor),
        mesh=fine,
        in_specs=(spec, spec),
        out_specs=(spec, spec),
        check_vma=False,
    )
```

```python
import functools

import jax
import jax.numpy as jnp
import numpy as np
from jax import lax
from jax.experimental import pallas as pl
from jax.experimental.pallas import tpu as pltpu
from jax.sharding import Mesh
from jax.sharding import PartitionSpec as P

AXES = ("groups", "z", "y", "c")
BLOCK = 16
LANES = 128
WINDOW = 4
SWAP = [(0, 1), (1, 0)]


def chunks_of(per_plane):
    unit = per_plane // 16
    sizes = [4 * unit, 5 * unit, 5 * unit, 2 * unit] if unit else [1] * per_plane
    return [(sum(sizes[:i]), size) for i, size in enumerate(sizes)]


def nt_dot(a, b):
    return lax.dot_general(a, b, (((1,), (1,)), ((), ())), preferred_element_type=jnp.float32)


def tn_dot(a, b):
    return lax.dot_general(a, b, (((0,), (0,)), ((), ())), preferred_element_type=jnp.float32)


def after(value, *others):
    return lax.optimization_barrier((value, others))[0]


def unfold_kernel(planes, per_plane, chunks, extra, z_ref, *refs):
    ins, factor, outs, wide = refs[:planes], refs[planes], refs[planes + 1 : -1], refs[-1]
    rows, _, cells = ins[0].shape
    for shift in range(planes):
        first = lax.rem(lax.rem(z_ref[0] + shift, planes) * per_plane, BLOCK)
        for h in range(0, cells, LANES):
            wide[...] = ins[shift][:, :, h : h + LANES].astype(jnp.float32).reshape(rows * BLOCK, LANES)
            for n, (start, size) in enumerate(chunks):
                out = outs[n * planes + shift]
                for s in range(size):
                    taken = wide[pl.ds(first + start + s, rows, stride=BLOCK), :]
                    out[:, s * cells + h : s * cells + h + LANES] = taken.astype(jnp.bfloat16)
        if extra is not None:
            outs[extra * planes + shift][:, chunks[extra][1] * cells :] = factor[...]


def unfold(slab, factor, z, planes, chunks, extra):
    rows, species, cells = slab.shape
    rank = factor.shape[1]
    per_plane = species // planes
    step = min(rows, 32)
    widths = [size * cells + (rank if n == extra else 0) for n, (_, size) in enumerate(chunks)]
    in_specs = [
        pl.BlockSpec(
            (step, BLOCK, cells),
            lambda i, z_ref, shift=shift: (i, lax.div(lax.rem(z_ref[0] + shift, planes) * per_plane, BLOCK), 0),
        )
        for shift in range(planes)
    ]
    in_specs.append(pl.BlockSpec((step, rank), lambda i, z_ref: (i, 0)))
    out = pl.pallas_call(
        functools.partial(unfold_kernel, planes, per_plane, chunks, extra),
        out_shape=[jax.ShapeDtypeStruct((rows, width), slab.dtype) for width in widths for _ in range(planes)],
        grid_spec=pltpu.PrefetchScalarGridSpec(
            num_scalar_prefetch=1,
            grid=(rows // step,),
            in_specs=in_specs,
            out_specs=[pl.BlockSpec((step, width), lambda i, z_ref: (i, 0)) for width in widths for _ in range(planes)],
            scratch_shapes=[pltpu.VMEM((step * BLOCK, LANES), jnp.float32)],
        ),
        compiler_params=pltpu.CompilerParams(vmem_limit_bytes=24 * 2**20),
        cost_estimate=pl.CostEstimate(
            flops=0, bytes_accessed=planes * rows * (BLOCK * cells + sum(widths)) * 2, transcendentals=0
        ),
        name="unfold",
    )(z.reshape(1).astype(jnp.int32), *([slab] * planes), factor)
    return [out[n * planes : (n + 1) * planes] for n in range(len(chunks))]


def finish_kernel(planes, scale, place_ref, *refs):
    out = refs[-1]
    rows = out.shape[0]
    sums = []
    for pair in range(2):
        own, below, above = refs[3 * pair : 3 * pair + 3]
        sums.append((own[...] + below[...] + above[...]) * scale)

    def block(k, z):
        at = ((k % 2) * planes + z) * rows
        return sums[k // 2][:, at : at + rows]

    for place in range(4):

        @pl.when(place_ref[0] == place)
        def _():
            for z in range(planes):
                pieces = [block(place ^ other, z) for other in range(4)]
                out[:, z * 4 * rows : (z + 1) * 4 * rows] = jnp.concatenate(pieces, axis=1)


def finish(planes, total, place, parts):
    rows = parts[0].shape[0]
    return pl.pallas_call(
        functools.partial(finish_kernel, planes, 1.0 / total),
        out_shape=jax.ShapeDtypeStruct((rows, 4 * planes * rows), jnp.float32),
        in_specs=[pl.BlockSpec(memory_space=pltpu.SMEM)] + [pl.BlockSpec(memory_space=pltpu.VMEM)] * len(parts),
        out_specs=pl.BlockSpec(memory_space=pltpu.VMEM),
        compiler_params=pltpu.CompilerParams(vmem_limit_bytes=24 * 2**20),
        name="finish",
    )(place.reshape(1).astype(jnp.int32), *parts)


def chain(planes, z, sums, up):
    rows = sums.shape[0] // planes
    got = first = None
    for step in range(1, planes):
        plane = planes - step + z if up else z - planes + step
        sent = lax.dynamic_slice_in_dim(sums, jnp.clip(plane, 0, planes - 1) * rows, rows, 0)
        if got is not None:
            sent = sent + got
        pairs = [(i, i + 1) for i in range(step)] if up else [(planes - 1 - i, planes - 2 - i) for i in range(step)]
        got = lax.ppermute(sent, "z", pairs)
        first = got if first is None else first
    return got, first


def on_device(planes, slab, factor):
    rows, species, cells = slab.shape
    rank = factor.shape[1]
    total = species * cells
    z, y, c = (lax.axis_index(name) for name in ("z", "y", "c"))
    place = y * 2 + c
    per_plane = species // planes
    chunks = chunks_of(per_plane)
    last = len(chunks) - 1
    pieces = unfold(slab, factor, z, planes, chunks[:1], None)
    pieces += unfold(slab, after(factor, pieces[0]), z, planes, chunks[1:], 0)

    def stacked(parts):
        stack = jnp.zeros((planes,) + parts[0].shape, slab.dtype)
        for shift in range(planes):
            stack = lax.dynamic_update_slice(stack, parts[shift][None], ((z - shift) % planes, 0, 0))
        return stack.reshape(planes * rows, -1)

    sent, waits, held = [], [], []
    for j in range(last + 1):
        arrived = [pieces[j][0]]
        for shift in range(1, planes):
            piece = pieces[j][shift]
            if len(sent) >= WINDOW:
                piece = after(piece, sent[-WINDOW], *(waits[min(j, last - 1) - 2] if j > 1 else ()))
            sent.append(lax.ppermute(piece, "z", [(s, (s + shift) % planes) for s in range(planes)]))
            arrived.append(sent[-1])
        stack = stacked(arrived)
        across = lax.ppermute(stack, "y", SWAP)
        beside = lax.ppermute(stack, "c", SWAP)
        waits.append((across, beside))
        held.append([stack, beside, across])
    flat = [[b[:, : size * cells] for b in held[j][:2]] for j, (_, size) in enumerate(chunks)]
    sums = [sum(nt_dot(flat[j][0], flat[j][k]) for j in range(last + 1)) for k in range(2)]
    parts, gate = [], None
    for half in range(2):
        if half:
            for j in range(last + 1):
                across = after(held[j][2], *gate) if j >= last - 1 else held[j][2]
                held[j].append(lax.ppermute(across, "c", SWAP))
                flat[j] += [b[:, : chunks[j][1] * cells] for b in held[j][2:]]
            sums = [sum(nt_dot(flat[j][0], flat[j][k]) for j in range(last + 1)) for k in range(2, 4)]
        both = jnp.concatenate(sums, axis=1)
        up, first_up = chain(planes, z, both, True)
        down, first_down = chain(planes, z, both, False)
        gate = (first_up, first_down)
        parts += [lax.dynamic_slice_in_dim(both, z * rows, rows, 0), up, down]
    factors = after([b[:, chunks[1][1] * cells :] for b in held[1]], *gate)
    gram = finish(planes, total, place, parts)
    own = per_plane // 4
    whole = [sum(tn_dot(flat[j][k], factors[k]) for k in range(4)) for j in range(last + 1)]
    whole = jnp.concatenate(whole, axis=0)
    core = lax.dynamic_slice_in_dim(whole, place * own * cells, own * cells, 0)
    return (gram, core)


def solution(mesh):
    groups, n = mesh.devices.shape
    planes = n // 4
    fine = Mesh(np.reshape(mesh.devices, (groups, planes, 2, 2)), AXES)
    spec = P(AXES)
    return jax.shard_map(
        lambda slab, factor: on_device(planes, slab, factor),
        mesh=fine,
        in_specs=(spec, spec),
        out_specs=(spec, spec),
        check_vma=False,
    )
```

```python
import functools

import jax
import jax.numpy as jnp
import numpy as np
from jax import lax
from jax.experimental import pallas as pl
from jax.experimental.pallas import tpu as pltpu
from jax.sharding import Mesh
from jax.sharding import PartitionSpec as P

AXES = ("groups", "z", "y", "c")
BLOCK = 16
LANES = 128
WINDOW = 4
SWAP = [(0, 1), (1, 0)]


def chunks_of(per_plane):
    unit = per_plane // 16
    sizes = [4 * unit, 4 * unit, 4 * unit, 2 * unit, 2 * unit] if unit else [1] * per_plane
    return [(sum(sizes[:i]), size) for i, size in enumerate(sizes)]


def nt_dot(a, b):
    return lax.dot_general(a, b, (((1,), (1,)), ((), ())), preferred_element_type=jnp.float32)


def tn_dot(a, b):
    return lax.dot_general(a, b, (((0,), (0,)), ((), ())), preferred_element_type=jnp.float32)


def after(value, *others):
    return lax.optimization_barrier((value, others))[0]


def unfold_kernel(planes, per_plane, chunks, extra, z_ref, *refs):
    ins, factor, outs, wide = refs[:planes], refs[planes], refs[planes + 1 : -1], refs[-1]
    rows, _, cells = ins[0].shape
    for shift in range(planes):
        first = lax.rem(lax.rem(z_ref[0] + shift, planes) * per_plane, BLOCK)
        for h in range(0, cells, LANES):
            wide[...] = ins[shift][:, :, h : h + LANES].astype(jnp.float32).reshape(rows * BLOCK, LANES)
            for n, (start, size) in enumerate(chunks):
                out = outs[n * planes + shift]
                for s in range(size):
                    taken = wide[pl.ds(first + start + s, rows, stride=BLOCK), :]
                    out[:, s * cells + h : s * cells + h + LANES] = taken.astype(jnp.bfloat16)
        if extra is not None:
            outs[extra * planes + shift][:, chunks[extra][1] * cells :] = factor[...]


def unfold(slab, factor, z, planes, chunks, extra):
    rows, species, cells = slab.shape
    rank = factor.shape[1]
    per_plane = species // planes
    step = min(rows, 32)
    widths = [size * cells + (rank if n == extra else 0) for n, (_, size) in enumerate(chunks)]
    in_specs = [
        pl.BlockSpec(
            (step, BLOCK, cells),
            lambda i, z_ref, shift=shift: (i, lax.div(lax.rem(z_ref[0] + shift, planes) * per_plane, BLOCK), 0),
        )
        for shift in range(planes)
    ]
    in_specs.append(pl.BlockSpec((step, rank), lambda i, z_ref: (i, 0)))
    out = pl.pallas_call(
        functools.partial(unfold_kernel, planes, per_plane, chunks, extra),
        out_shape=[jax.ShapeDtypeStruct((rows, width), slab.dtype) for width in widths for _ in range(planes)],
        grid_spec=pltpu.PrefetchScalarGridSpec(
            num_scalar_prefetch=1,
            grid=(rows // step,),
            in_specs=in_specs,
            out_specs=[pl.BlockSpec((step, width), lambda i, z_ref: (i, 0)) for width in widths for _ in range(planes)],
            scratch_shapes=[pltpu.VMEM((step * BLOCK, LANES), jnp.float32)],
        ),
        compiler_params=pltpu.CompilerParams(vmem_limit_bytes=24 * 2**20),
        cost_estimate=pl.CostEstimate(
            flops=0, bytes_accessed=planes * rows * (BLOCK * cells + sum(widths)) * 2, transcendentals=0
        ),
        name="unfold",
    )(z.reshape(1).astype(jnp.int32), *([slab] * planes), factor)
    return [out[n * planes : (n + 1) * planes] for n in range(len(chunks))]


def finish_kernel(planes, scale, at_ref, *refs):
    out = refs[-1]
    rows = out.shape[0]
    half = planes // 2
    each = 2 * half
    z, place = at_ref[0], at_ref[1]

    def put(k, plane, value):
        at = (lax.rem(plane, planes) * 4 + (place ^ k)) * rows
        out[:, pl.ds(pl.multiple_of(at, LANES), rows)] = value * scale

    for h in range(2):
        own, others = refs[each * h], refs[each * h + 1 : each * (h + 1)]
        for n in range(2):
            k = 2 * h + n
            for e in range(half):
                at = (n * half + e) * rows
                put(k, z + e, own[:, at : at + rows])
                if e:
                    put(k, z + planes - e, others[n * (half - 1) + e - 1][...].T)
        lower = (z < half).astype(jnp.int32)
        put(2 * h + 1 - lower, z + half, own[:, 2 * half * rows :])
        put(2 * h + lower, z + half, others[-1][...].T)


def finish(planes, total, z, place, parts):
    rows = parts[0].shape[0]
    half = planes // 2
    if rows % LANES == 0:
        return pl.pallas_call(
            functools.partial(finish_kernel, planes, 1.0 / total),
            out_shape=jax.ShapeDtypeStruct((rows, 4 * planes * rows), jnp.float32),
            in_specs=[pl.BlockSpec(memory_space=pltpu.SMEM)] + [pl.BlockSpec(memory_space=pltpu.VMEM)] * len(parts),
            out_specs=pl.BlockSpec(memory_space=pltpu.VMEM),
            compiler_params=pltpu.CompilerParams(vmem_limit_bytes=24 * 2**20),
            name="finish",
        )(jnp.stack([z, place]).astype(jnp.int32), *parts)
    each = 2 * half
    blocks = {}
    for h in range(2):
        own, others = parts[each * h], parts[each * h + 1 : each * (h + 1)]
        for n in range(2):
            for e in range(half):
                at = (n * half + e) * rows
                blocks[e, 2 * h + n] = own[:, at : at + rows]
                if e:
                    blocks[planes - e, 2 * h + n] = others[n * (half - 1) + e - 1].T
        last, got = own[:, 2 * half * rows :], others[-1].T
        blocks[half, 2 * h] = jnp.where(z < half, last, got)
        blocks[half, 2 * h + 1] = jnp.where(z < half, got, last)
    near = jnp.stack([blocks[e, k] for e in range(planes) for k in range(4)])
    column = jnp.arange(4 * planes)
    near = jnp.take(near, (column // 4 - z) % planes * 4 + (column % 4 ^ place), axis=0)
    return near.transpose(1, 0, 2).reshape(rows, -1) * (1.0 / total)


def halves(planes, pair):
    rows = pair[0].shape[0] // planes
    half = planes // 2
    out = []
    for plane in range(planes):
        own = [p[plane * rows : (plane + 1) * rows] for p in pair]
        pieces = []
        for p in own:
            if plane + half <= planes:
                pieces.append(p[:, plane * rows : (plane + half) * rows])
            else:
                pieces += [p[:, plane * rows :], p[:, : (plane + half - planes) * rows]]
        far = (plane + half) % planes * rows
        pieces.append(own[plane // half][:, far : far + rows])
        out.append(jnp.concatenate(pieces, axis=1))
    return jnp.stack(out)


def mirror(planes, h, sums):
    rows = sums.shape[0]
    half = planes // 2
    axes = ("z", "y", "c")
    got = []
    for n in range(2):
        for e in range(1, half):
            at = (n * half + e) * rows
            pairs = [(4 * i + a, (i + e) % planes * 4 + (a ^ (2 * h + n))) for i in range(planes) for a in range(4)]
            got.append(lax.ppermute(sums[:, at : at + rows], axes, pairs))
    pairs = [(4 * i + a, (i + half) % planes * 4 + (a ^ (2 * h + i // half))) for i in range(planes) for a in range(4)]
    got.append(lax.ppermute(sums[:, 2 * half * rows :], axes, pairs))
    return got


def chain(planes, z, sums, up):
    got = early = None
    for step in range(1, planes):
        plane = planes - step + z if up else z - planes + step
        sent = lax.dynamic_index_in_dim(sums, jnp.clip(plane, 0, planes - 1), 0, keepdims=False)
        if got is not None:
            sent = sent + got
        pairs = [(i, i + 1) for i in range(step)] if up else [(planes - 1 - i, planes - 2 - i) for i in range(step)]
        got = lax.ppermute(sent, "z", pairs)
        early = got if step < 3 else early
    return got, early


def on_device(planes, slab, factor):
    rows, species, cells = slab.shape
    rank = factor.shape[1]
    total = species * cells
    z, y, c = (lax.axis_index(name) for name in ("z", "y", "c"))
    place = y * 2 + c
    per_plane = species // planes
    chunks = chunks_of(per_plane)
    last = len(chunks) - 1
    pieces = unfold(slab, factor, z, planes, chunks[:1], None)
    pieces += unfold(slab, after(factor, pieces[0]), z, planes, chunks[1:], 0)

    def stacked(parts):
        stack = jnp.zeros((planes,) + parts[0].shape, slab.dtype)
        for shift in range(planes):
            stack = lax.dynamic_update_slice(stack, parts[shift][None], ((z - shift) % planes, 0, 0))
        return stack.reshape(planes * rows, -1)

    sent, waits, held = [], [], []
    for j in range(last + 1):
        arrived = [pieces[j][0]]
        for shift in range(1, planes):
            piece = pieces[j][shift]
            if len(sent) >= WINDOW:
                piece = after(
                    piece,
                    sent[-WINDOW],
                    *(waits[min(j, last - 1) - 2] if j > 1 else ()),
                    *(held[j - 3][3:] if j > 2 else ()),
                )
            sent.append(lax.ppermute(piece, "z", [(s, (s + shift) % planes) for s in range(planes)]))
            arrived.append(sent[-1])
        stack = stacked(arrived)
        across = lax.ppermute(stack, "y", SWAP)
        beside = lax.ppermute(stack, "c", SWAP)
        waits.append((across, beside))
        held.append([stack, beside, across])
        if j < last - 2:
            held[j].append(lax.ppermute(across, "c", SWAP))
    flat = [[b[:, : size * cells] for b in held[j][:2]] for j, (_, size) in enumerate(chunks)]
    sums = [sum(nt_dot(flat[j][0], flat[j][k]) for j in range(last + 1)) for k in range(2)]
    parts, gate = [], None
    for half in range(2):
        if half:
            for j in range(last + 1):
                if j >= last - 2:
                    held[j][2] = after(held[j][2], *gate)
                    held[j].append(lax.ppermute(held[j][2], "c", SWAP))
                flat[j] += [b[:, : chunks[j][1] * cells] for b in held[j][2:]]
            sums = [sum(nt_dot(flat[j][0], flat[j][k]) for j in range(last + 1)) for k in range(2, 4)]
        both = halves(planes, sums)
        up, early_up = chain(planes, z, both, True)
        down, early_down = chain(planes, z, both, False)
        gate = (early_up, early_down)
        whole = lax.dynamic_index_in_dim(both, z, 0, keepdims=False) + up + down
        parts += [whole, *mirror(planes, half, whole)]
    factors = [b[:, chunks[1][1] * cells :] for b in held[1]]
    gram = finish(planes, total, z, place, parts)
    own = per_plane // 4
    whole = [sum(tn_dot(flat[j][k], factors[k]) for k in range(4)) for j in range(last + 1)]
    whole = jnp.concatenate(whole, axis=0)
    core = lax.dynamic_slice_in_dim(whole, place * own * cells, own * cells, 0)
    return (gram, core)


def solution(mesh):
    groups, n = mesh.devices.shape
    planes = n // 4
    fine = Mesh(np.reshape(mesh.devices, (groups, planes, 2, 2)), AXES)
    spec = P(AXES)
    return jax.shard_map(
        lambda slab, factor: on_device(planes, slab, factor),
        mesh=fine,
        in_specs=(spec, spec),
        out_specs=(spec, spec),
        check_vma=False,
    )
```

```python
import functools

import jax
import jax.numpy as jnp
import numpy as np
from jax import lax
from jax.experimental import pallas as pl
from jax.experimental.pallas import tpu as pltpu
from jax.sharding import Mesh
from jax.sharding import PartitionSpec as P

AXES = ("groups", "z", "y", "c")
BLOCK = 16
LANES = 128
WINDOW = 4
SWAP = [(0, 1), (1, 0)]


def chunks_of(per_plane):
    unit = per_plane // 16
    sizes = [4 * unit, 5 * unit, 5 * unit, 2 * unit] if unit else [1] * per_plane
    return [(sum(sizes[:i]), size) for i, size in enumerate(sizes)]


def nt_dot(a, b):
    return lax.dot_general(a, b, (((1,), (1,)), ((), ())), preferred_element_type=jnp.float32)


def tn_dot(a, b):
    return lax.dot_general(a, b, (((0,), (0,)), ((), ())), preferred_element_type=jnp.float32)


def after(value, *others):
    return lax.optimization_barrier((value, others))[0]


def unfold_kernel(planes, per_plane, chunks, extra, z_ref, *refs):
    ins, factor, outs, wide = refs[:planes], refs[planes], refs[planes + 1 : -1], refs[-1]
    rows, _, cells = ins[0].shape
    for shift in range(planes):
        first = lax.rem(lax.rem(z_ref[0] + shift, planes) * per_plane, BLOCK)
        for h in range(0, cells, LANES):
            wide[...] = ins[shift][:, :, h : h + LANES].astype(jnp.float32).reshape(rows * BLOCK, LANES)
            for n, (start, size) in enumerate(chunks):
                out = outs[n * planes + shift]
                for s in range(size):
                    taken = wide[pl.ds(first + start + s, rows, stride=BLOCK), :]
                    out[:, s * cells + h : s * cells + h + LANES] = taken.astype(jnp.bfloat16)
        if extra is not None:
            outs[extra * planes + shift][:, chunks[extra][1] * cells :] = factor[...]


def unfold(slab, factor, z, planes, chunks, extra):
    rows, species, cells = slab.shape
    rank = factor.shape[1]
    per_plane = species // planes
    step = min(rows, 32)
    widths = [size * cells + (rank if n == extra else 0) for n, (_, size) in enumerate(chunks)]
    in_specs = [
        pl.BlockSpec(
            (step, BLOCK, cells),
            lambda i, z_ref, shift=shift: (i, lax.div(lax.rem(z_ref[0] + shift, planes) * per_plane, BLOCK), 0),
        )
        for shift in range(planes)
    ]
    in_specs.append(pl.BlockSpec((step, rank), lambda i, z_ref: (i, 0)))
    out = pl.pallas_call(
        functools.partial(unfold_kernel, planes, per_plane, chunks, extra),
        out_shape=[jax.ShapeDtypeStruct((rows, width), slab.dtype) for width in widths for _ in range(planes)],
        grid_spec=pltpu.PrefetchScalarGridSpec(
            num_scalar_prefetch=1,
            grid=(rows // step,),
            in_specs=in_specs,
            out_specs=[pl.BlockSpec((step, width), lambda i, z_ref: (i, 0)) for width in widths for _ in range(planes)],
            scratch_shapes=[pltpu.VMEM((step * BLOCK, LANES), jnp.float32)],
        ),
        compiler_params=pltpu.CompilerParams(vmem_limit_bytes=24 * 2**20),
        cost_estimate=pl.CostEstimate(
            flops=0, bytes_accessed=planes * rows * (BLOCK * cells + sum(widths)) * 2, transcendentals=0
        ),
        name="unfold",
    )(z.reshape(1).astype(jnp.int32), *([slab] * planes), factor)
    return [out[n * planes : (n + 1) * planes] for n in range(len(chunks))]


def finish_kernel(planes, scale, place_ref, *refs):
    out = refs[-1]
    rows = out.shape[0]
    sums = []
    for pair in range(2):
        own, below, above = refs[3 * pair : 3 * pair + 3]
        sums.append((own[...] + below[...] + above[...]) * scale)

    def block(k, z):
        at = ((k % 2) * planes + z) * rows
        return sums[k // 2][:, at : at + rows]

    for place in range(4):

        @pl.when(place_ref[0] == place)
        def _():
            for z in range(planes):
                pieces = [block(place ^ other, z) for other in range(4)]
                out[:, z * 4 * rows : (z + 1) * 4 * rows] = jnp.concatenate(pieces, axis=1)


def finish(planes, total, place, parts):
    rows = parts[0].shape[0]
    return pl.pallas_call(
        functools.partial(finish_kernel, planes, 1.0 / total),
        out_shape=jax.ShapeDtypeStruct((rows, 4 * planes * rows), jnp.float32),
        in_specs=[pl.BlockSpec(memory_space=pltpu.SMEM)] + [pl.BlockSpec(memory_space=pltpu.VMEM)] * len(parts),
        out_specs=pl.BlockSpec(memory_space=pltpu.VMEM),
        compiler_params=pltpu.CompilerParams(vmem_limit_bytes=24 * 2**20),
        name="finish",
    )(place.reshape(1).astype(jnp.int32), *parts)


def chain(planes, z, sums, up, ahead):
    rows = sums.shape[0] // planes
    got = early = None
    for step in range(1, planes):
        plane = planes - step + z if up else z - planes + step
        sent = lax.dynamic_slice_in_dim(sums, jnp.clip(plane, 0, planes - 1) * rows, rows, 0)
        if got is not None:
            sent = sent + (after(got, *ahead) if step == 2 else got)
        pairs = [(i, i + 1) for i in range(step)] if up else [(planes - 1 - i, planes - 2 - i) for i in range(step)]
        early = sent if step < 4 else early
        got = lax.ppermute(sent, "z", pairs)
    return got, early


def on_device(planes, slab, factor):
    rows, species, cells = slab.shape
    rank = factor.shape[1]
    total = species * cells
    z, y, c = (lax.axis_index(name) for name in ("z", "y", "c"))
    place = y * 2 + c
    per_plane = species // planes
    chunks = chunks_of(per_plane)
    last = len(chunks) - 1
    pieces = unfold(slab, factor, z, planes, chunks[:1], None)
    pieces += unfold(slab, after(factor, pieces[0]), z, planes, chunks[1:], 0)

    def stacked(parts):
        stack = jnp.zeros((planes,) + parts[0].shape, slab.dtype)
        for shift in range(planes):
            stack = lax.dynamic_update_slice(stack, parts[shift][None], ((z - shift) % planes, 0, 0))
        return stack.reshape(planes * rows, -1)

    sent, waits, held = [], [], []
    for j in range(last + 1):
        arrived = [pieces[j][0]]
        for shift in range(1, planes):
            piece = pieces[j][shift]
            if len(sent) >= WINDOW:
                piece = after(
                    piece,
                    sent[-WINDOW],
                    *(waits[min(j, last - 1) - 2] if j > 1 else ()),
                    *(held[j - 3][3:] if j > 2 else ()),
                )
            sent.append(lax.ppermute(piece, "z", [(s, (s + shift) % planes) for s in range(planes)]))
            arrived.append(sent[-1])
        stack = stacked(arrived)
        across = lax.ppermute(stack, "y", SWAP)
        beside = lax.ppermute(stack, "c", SWAP)
        waits.append((across, beside))
        held.append([stack, beside, across])
        if j < last - 1:
            held[j].append(lax.ppermute(across, "c", SWAP))
    flat = [[b[:, : size * cells] for b in held[j][:2]] for j, (_, size) in enumerate(chunks)]
    sums = [sum(nt_dot(flat[j][0], flat[j][k]) for j in range(last + 1)) for k in range(2)]
    parts, gate = [], None
    for half in range(2):
        if half:
            for j in range(last + 1):
                if j >= last - 1:
                    held[j][2] = after(held[j][2], *gate)
                    held[j].append(lax.ppermute(held[j][2], "c", SWAP))
                flat[j] += [b[:, : chunks[j][1] * cells] for b in held[j][2:]]
            sums = [sum(nt_dot(flat[j][0], flat[j][k]) for j in range(last + 1)) for k in range(2, 4)]
        both = jnp.concatenate(sums, axis=1)
        up, early_up = chain(planes, z, both, True, parts[1:3])
        down, early_down = chain(planes, z, both, False, parts[1:3])
        gate = (early_up, early_down)
        parts += [lax.dynamic_slice_in_dim(both, z * rows, rows, 0), up, down]
    factors = [b[:, chunks[1][1] * cells :] for b in held[1]]
    gram = finish(planes, total, place, parts)
    own = per_plane // 4
    whole = [sum(tn_dot(flat[j][k], factors[k]) for k in range(4)) for j in range(last + 1)]
    whole = jnp.concatenate(whole, axis=0)
    core = lax.dynamic_slice_in_dim(whole, place * own * cells, own * cells, 0)
    return (gram, core)


def solution(mesh):
    groups, n = mesh.devices.shape
    planes = n // 4
    fine = Mesh(np.reshape(mesh.devices, (groups, planes, 2, 2)), AXES)
    spec = P(AXES)
    return jax.shard_map(
        lambda slab, factor: on_device(planes, slab, factor),
        mesh=fine,
        in_specs=(spec, spec),
        out_specs=(spec, spec),
        check_vma=False,
    )
```

```python
import functools

import jax
import jax.numpy as jnp
import numpy as np
from jax import lax
from jax.experimental import pallas as pl
from jax.experimental.pallas import tpu as pltpu
from jax.sharding import Mesh
from jax.sharding import PartitionSpec as P

AXES = ("groups", "z", "y", "c")
BLOCK = 16
LANES = 128
WINDOW = 4
SWAP = [(0, 1), (1, 0)]


def chunks_of(per_plane):
    unit = per_plane // 16
    sizes = [4 * unit, 4 * unit, 4 * unit, 2 * unit, 2 * unit] if unit else [1] * per_plane
    return [(sum(sizes[:i]), size) for i, size in enumerate(sizes)]


def nt_dot(a, b):
    return lax.dot_general(a, b, (((1,), (1,)), ((), ())), preferred_element_type=jnp.float32)


def tn_dot(a, b):
    return lax.dot_general(a, b, (((0,), (0,)), ((), ())), preferred_element_type=jnp.float32)


def after(value, *others):
    return lax.optimization_barrier((value, others))[0]


def unfold_kernel(planes, per_plane, chunks, extra, z_ref, *refs):
    ins, factor, outs, wide = refs[:planes], refs[planes], refs[planes + 1 : -1], refs[-1]
    rows, _, cells = ins[0].shape
    for shift in range(planes):
        first = lax.rem(lax.rem(z_ref[0] + shift, planes) * per_plane, BLOCK)
        for h in range(0, cells, LANES):
            wide[...] = ins[shift][:, :, h : h + LANES].astype(jnp.float32).reshape(rows * BLOCK, LANES)
            for n, (start, size) in enumerate(chunks):
                out = outs[n * planes + shift]
                for s in range(size):
                    taken = wide[pl.ds(first + start + s, rows, stride=BLOCK), :]
                    out[:, s * cells + h : s * cells + h + LANES] = taken.astype(jnp.bfloat16)
        if extra is not None:
            outs[extra * planes + shift][:, chunks[extra][1] * cells :] = factor[...]


def unfold(slab, factor, z, planes, chunks, extra):
    rows, species, cells = slab.shape
    rank = factor.shape[1]
    per_plane = species // planes
    step = min(rows, 32)
    widths = [size * cells + (rank if n == extra else 0) for n, (_, size) in enumerate(chunks)]
    in_specs = [
        pl.BlockSpec(
            (step, BLOCK, cells),
            lambda i, z_ref, shift=shift: (i, lax.div(lax.rem(z_ref[0] + shift, planes) * per_plane, BLOCK), 0),
        )
        for shift in range(planes)
    ]
    in_specs.append(pl.BlockSpec((step, rank), lambda i, z_ref: (i, 0)))
    out = pl.pallas_call(
        functools.partial(unfold_kernel, planes, per_plane, chunks, extra),
        out_shape=[jax.ShapeDtypeStruct((rows, width), slab.dtype) for width in widths for _ in range(planes)],
        grid_spec=pltpu.PrefetchScalarGridSpec(
            num_scalar_prefetch=1,
            grid=(rows // step,),
            in_specs=in_specs,
            out_specs=[pl.BlockSpec((step, width), lambda i, z_ref: (i, 0)) for width in widths for _ in range(planes)],
            scratch_shapes=[pltpu.VMEM((step * BLOCK, LANES), jnp.float32)],
        ),
        compiler_params=pltpu.CompilerParams(vmem_limit_bytes=24 * 2**20),
        cost_estimate=pl.CostEstimate(
            flops=0, bytes_accessed=planes * rows * (BLOCK * cells + sum(widths)) * 2, transcendentals=0
        ),
        name="unfold",
    )(z.reshape(1).astype(jnp.int32), *([slab] * planes), factor)
    return [out[n * planes : (n + 1) * planes] for n in range(len(chunks))]


def finish_kernel(planes, scale, place_ref, *refs):
    out = refs[-1]
    rows = out.shape[0]
    sums = []
    for pair in range(2):
        own, below, above = refs[3 * pair : 3 * pair + 3]
        sums.append((own[...] + below[...] + above[...]) * scale)

    def block(k, z):
        at = ((k % 2) * planes + z) * rows
        return sums[k // 2][:, at : at + rows]

    for place in range(4):

        @pl.when(place_ref[0] == place)
        def _():
            for z in range(planes):
                pieces = [block(place ^ other, z) for other in range(4)]
                out[:, z * 4 * rows : (z + 1) * 4 * rows] = jnp.concatenate(pieces, axis=1)


def finish(planes, total, place, parts):
    rows = parts[0].shape[0]
    return pl.pallas_call(
        functools.partial(finish_kernel, planes, 1.0 / total),
        out_shape=jax.ShapeDtypeStruct((rows, 4 * planes * rows), jnp.float32),
        in_specs=[pl.BlockSpec(memory_space=pltpu.SMEM)] + [pl.BlockSpec(memory_space=pltpu.VMEM)] * len(parts),
        out_specs=pl.BlockSpec(memory_space=pltpu.VMEM),
        compiler_params=pltpu.CompilerParams(vmem_limit_bytes=24 * 2**20),
        name="finish",
    )(place.reshape(1).astype(jnp.int32), *parts)


def chain(planes, z, sums, up):
    rows = sums.shape[0] // planes
    got = first = None
    for step in range(1, planes):
        plane = planes - step + z if up else z - planes + step
        sent = lax.dynamic_slice_in_dim(sums, jnp.clip(plane, 0, planes - 1) * rows, rows, 0)
        if got is not None:
            sent = sent + got
        pairs = [(i, i + 1) for i in range(step)] if up else [(planes - 1 - i, planes - 2 - i) for i in range(step)]
        got = lax.ppermute(sent, "z", pairs)
        first = got if first is None else first
    return got, first


def on_device(planes, slab, factor):
    rows, species, cells = slab.shape
    rank = factor.shape[1]
    total = species * cells
    z, y, c = (lax.axis_index(name) for name in ("z", "y", "c"))
    place = y * 2 + c
    per_plane = species // planes
    chunks = chunks_of(per_plane)
    last = len(chunks) - 1
    pieces = unfold(slab, factor, z, planes, chunks[:1], None)
    pieces += unfold(slab, after(factor, pieces[0]), z, planes, chunks[1:], 0)

    def stacked(parts):
        stack = jnp.zeros((planes,) + parts[0].shape, slab.dtype)
        for shift in range(planes):
            stack = lax.dynamic_update_slice(stack, parts[shift][None], ((z - shift) % planes, 0, 0))
        return stack.reshape(planes * rows, -1)

    sent, waits, held = [], [], []
    for j in range(last + 1):
        arrived = [pieces[j][0]]
        for shift in range(1, planes):
            piece = pieces[j][shift]
            if len(sent) >= WINDOW:
                piece = after(
                    piece,
                    sent[-WINDOW],
                    *(waits[min(j, last - 1) - 2] if j > 1 else ()),
                    *(held[min(j, last - 1) - 3][3:] if j > 2 and last > 3 else ()),
                    *((held[j - 3][3], held[j - 2][1]) if j == last > 3 and shift == planes - 1 else ()),
                )
            sent.append(lax.ppermute(piece, "z", [(s, (s + shift) % planes) for s in range(planes)]))
            arrived.append(sent[-1])
        stack = stacked(arrived)
        across = lax.ppermute(stack, "y", SWAP)
        beside = lax.ppermute(stack, "c", SWAP)
        waits.append((across, beside))
        held.append([stack, beside, across])
        if j < last - 1:
            held[j].append(lax.ppermute(across, "c", SWAP))
    flat = [[b[:, : size * cells] for b in held[j][:2]] for j, (_, size) in enumerate(chunks)]
    sums = [sum(nt_dot(flat[j][0], flat[j][k]) for j in range(last + 1)) for k in range(2)]
    parts, gate = [], None
    for half in range(2):
        if half:
            for j in range(last + 1):
                if j >= last - 1:
                    held[j][2] = after(held[j][2], *gate)
                    held[j].append(lax.ppermute(held[j][2], "c", SWAP))
                flat[j] += [b[:, : chunks[j][1] * cells] for b in held[j][2:]]
            sums = [sum(nt_dot(flat[j][0], flat[j][k]) for j in range(last + 1)) for k in range(2, 4)]
        both = jnp.concatenate(sums, axis=1)
        up, first_up = chain(planes, z, both, True)
        down, first_down = chain(planes, z, both, False)
        gate = (first_up, first_down)
        parts += [lax.dynamic_slice_in_dim(both, z * rows, rows, 0), up, down]
    gram = finish(planes, total, place, parts)
    own = per_plane // 4

    def kept(mine, held):
        out = []
        for j, (start, size) in enumerate(chunks):
            low, high = max(start, mine * own) - start, min(start + size, (mine + 1) * own) - start
            if low < high:
                out.append(
                    sum(
                        tn_dot(held[j][k][:, low * cells : high * cells], held[1][k][:, chunks[1][1] * cells :])
                        for k in range(4)
                    )
                )
        return jnp.concatenate(out, axis=0)

    core = lax.switch(place, [functools.partial(kept, mine) for mine in range(4)], after(held, *gate))
    return (gram, core)


def solution(mesh):
    groups, n = mesh.devices.shape
    planes = n // 4
    fine = Mesh(np.reshape(mesh.devices, (groups, planes, 2, 2)), AXES)
    spec = P(AXES)
    return jax.shard_map(
        lambda slab, factor: on_device(planes, slab, factor),
        mesh=fine,
        in_specs=(spec, spec),
        out_specs=(spec, spec),
        check_vma=False,
    )
```

```python
import functools

import jax
import jax.numpy as jnp
import numpy as np
from jax import lax
from jax.experimental import pallas as pl
from jax.experimental.pallas import tpu as pltpu
from jax.sharding import Mesh
from jax.sharding import PartitionSpec as P

AXES = ("groups", "z", "y", "c")
BLOCK = 16
LANES = 128
WINDOW = 4
SWAP = [(0, 1), (1, 0)]


def chunks_of(per_plane):
    unit = per_plane // 16
    sizes = [6 * unit, 6 * unit, 4 * unit] if unit else [1] * per_plane
    return [(sum(sizes[:i]), size) for i, size in enumerate(sizes)]


def nt_dot(a, b):
    return lax.dot_general(a, b, (((1,), (1,)), ((), ())), preferred_element_type=jnp.float32)


def tn_dot(a, b):
    return lax.dot_general(a, b, (((0,), (0,)), ((), ())), preferred_element_type=jnp.float32)


def after(value, *others):
    return lax.optimization_barrier((value, others))[0]


def unfold_kernel(planes, per_plane, chunks, extra, z_ref, *refs):
    ins, factor, outs, wide = refs[:planes], refs[planes], refs[planes + 1 : -1], refs[-1]
    rows, _, cells = ins[0].shape
    for shift in range(planes):
        first = lax.rem(lax.rem(z_ref[0] + shift, planes) * per_plane, BLOCK)
        for h in range(0, cells, LANES):
            wide[...] = ins[shift][:, :, h : h + LANES].astype(jnp.float32).reshape(rows * BLOCK, LANES)
            for n, (start, size) in enumerate(chunks):
                out = outs[n * planes + shift]
                for s in range(size):
                    taken = wide[pl.ds(first + start + s, rows, stride=BLOCK), :]
                    out[:, s * cells + h : s * cells + h + LANES] = taken.astype(jnp.bfloat16)
        if extra is not None:
            outs[extra * planes + shift][:, chunks[extra][1] * cells :] = factor[...]


def unfold(slab, factor, z, planes, chunks, extra):
    rows, species, cells = slab.shape
    rank = factor.shape[1]
    per_plane = species // planes
    step = min(rows, 32)
    widths = [size * cells + (rank if n == extra else 0) for n, (_, size) in enumerate(chunks)]
    in_specs = [
        pl.BlockSpec(
            (step, BLOCK, cells),
            lambda i, z_ref, shift=shift: (i, lax.div(lax.rem(z_ref[0] + shift, planes) * per_plane, BLOCK), 0),
        )
        for shift in range(planes)
    ]
    in_specs.append(pl.BlockSpec((step, rank), lambda i, z_ref: (i, 0)))
    out = pl.pallas_call(
        functools.partial(unfold_kernel, planes, per_plane, chunks, extra),
        out_shape=[jax.ShapeDtypeStruct((rows, width), slab.dtype) for width in widths for _ in range(planes)],
        grid_spec=pltpu.PrefetchScalarGridSpec(
            num_scalar_prefetch=1,
            grid=(rows // step,),
            in_specs=in_specs,
            out_specs=[pl.BlockSpec((step, width), lambda i, z_ref: (i, 0)) for width in widths for _ in range(planes)],
            scratch_shapes=[pltpu.VMEM((step * BLOCK, LANES), jnp.float32)],
        ),
        compiler_params=pltpu.CompilerParams(vmem_limit_bytes=24 * 2**20),
        cost_estimate=pl.CostEstimate(
            flops=0, bytes_accessed=planes * rows * (BLOCK * cells + sum(widths)) * 2, transcendentals=0
        ),
        name="unfold",
    )(z.reshape(1).astype(jnp.int32), *([slab] * planes), factor)
    return [out[n * planes : (n + 1) * planes] for n in range(len(chunks))]


def finish_kernel(planes, scale, place_ref, *refs):
    out = refs[-1]
    rows = out.shape[0]
    sums = []
    for pair in range(2):
        own, below, above = refs[3 * pair : 3 * pair + 3]
        sums.append((own[...] + below[...] + above[...]) * scale)

    def block(k, z):
        at = ((k % 2) * planes + z) * rows
        return sums[k // 2][:, at : at + rows]

    for place in range(4):

        @pl.when(place_ref[0] == place)
        def _():
            for z in range(planes):
                pieces = [block(place ^ other, z) for other in range(4)]
                out[:, z * 4 * rows : (z + 1) * 4 * rows] = jnp.concatenate(pieces, axis=1)


def finish(planes, total, place, parts):
    rows = parts[0].shape[0]
    return pl.pallas_call(
        functools.partial(finish_kernel, planes, 1.0 / total),
        out_shape=jax.ShapeDtypeStruct((rows, 4 * planes * rows), jnp.float32),
        in_specs=[pl.BlockSpec(memory_space=pltpu.SMEM)] + [pl.BlockSpec(memory_space=pltpu.VMEM)] * len(parts),
        out_specs=pl.BlockSpec(memory_space=pltpu.VMEM),
        compiler_params=pltpu.CompilerParams(vmem_limit_bytes=24 * 2**20),
        name="finish",
    )(place.reshape(1).astype(jnp.int32), *parts)


def chain(planes, z, sums, up):
    rows = sums.shape[0] // planes
    got = first = None
    for step in range(1, planes):
        plane = planes - step + z if up else z - planes + step
        sent = lax.dynamic_slice_in_dim(sums, jnp.clip(plane, 0, planes - 1) * rows, rows, 0)
        if got is not None:
            sent = sent + got
        pairs = [(i, i + 1) for i in range(step)] if up else [(planes - 1 - i, planes - 2 - i) for i in range(step)]
        got = lax.ppermute(sent, "z", pairs)
        first = got if first is None else first
    return got, first


def on_device(planes, slab, factor):
    rows, species, cells = slab.shape
    rank = factor.shape[1]
    total = species * cells
    z, y, c = (lax.axis_index(name) for name in ("z", "y", "c"))
    place = y * 2 + c
    per_plane = species // planes
    chunks = chunks_of(per_plane)
    last = len(chunks) - 1
    pieces = unfold(slab, factor, z, planes, chunks[:1], None)
    pieces += unfold(slab, after(factor, pieces[0]), z, planes, chunks[1:], 0)

    def stacked(parts):
        stack = jnp.zeros((planes,) + parts[0].shape, slab.dtype)
        for shift in range(planes):
            stack = lax.dynamic_update_slice(stack, parts[shift][None], ((z - shift) % planes, 0, 0))
        return stack.reshape(planes * rows, -1)

    sent, waits, held = [], [], []
    for j in range(last + 1):
        arrived = [pieces[j][0] if j else after(pieces[0][0], pieces[1])]
        for shift in range(1, planes):
            piece = pieces[j][shift]
            if len(sent) >= WINDOW:
                piece = after(
                    piece,
                    sent[-WINDOW],
                    *(waits[j - 2] if j > 1 else ()),
                )
            sent.append(lax.ppermute(piece, "z", [(s, (s + shift) % planes) for s in range(planes)]))
            arrived.append(sent[-1])
        stack = stacked(arrived)
        across = lax.ppermute(stack, "y", SWAP)
        beside = lax.ppermute(stack, "c", SWAP)
        waits.append((across, beside))
        held.append([stack, beside, across])
        if j < last:
            held[j].append(lax.ppermute(across, "c", SWAP))
    flat = [[b[:, : size * cells] for b in held[j][:2]] for j, (_, size) in enumerate(chunks)]
    sums = [sum(nt_dot(flat[j][0], flat[j][k]) for j in range(last + 1)) for k in range(2)]
    parts, gate = [], None
    for half in range(2):
        if half:
            for j in range(last + 1):
                if j == last:
                    held[j][2] = after(held[j][2], *gate)
                    held[j].append(lax.ppermute(held[j][2], "c", SWAP))
                flat[j] += [b[:, : chunks[j][1] * cells] for b in held[j][2:]]
            sums = [sum(nt_dot(flat[j][0], flat[j][k]) for j in range(last + 1)) for k in range(2, 4)]
        both = jnp.concatenate(sums, axis=1)
        up, first_up = chain(planes, z, both, True)
        down, first_down = chain(planes, z, both, False)
        gate = (first_up, first_down)
        parts += [lax.dynamic_slice_in_dim(both, z * rows, rows, 0), up, down]
    gram = finish(planes, total, place, parts)
    own = per_plane // 4

    def kept(mine, held):
        out = []
        for j, (start, size) in enumerate(chunks):
            low, high = max(start, mine * own) - start, min(start + size, (mine + 1) * own) - start
            if low < high:
                out.append(
                    sum(
                        tn_dot(held[j][k][:, low * cells : high * cells], held[1][k][:, chunks[1][1] * cells :])
                        for k in range(4)
                    )
                )
        return jnp.concatenate(out, axis=0)

    core = lax.switch(place, [functools.partial(kept, mine) for mine in range(4)], after(held, *gate))
    return (gram, core)


def solution(mesh):
    groups, n = mesh.devices.shape
    planes = n // 4
    fine = Mesh(np.reshape(mesh.devices, (groups, planes, 2, 2)), AXES)
    spec = P(AXES)
    return jax.shard_map(
        lambda slab, factor: on_device(planes, slab, factor),
        mesh=fine,
        in_specs=(spec, spec),
        out_specs=(spec, spec),
        check_vma=False,
    )
```

```python
import functools

import jax
import jax.numpy as jnp
import numpy as np
from jax import lax
from jax.experimental import pallas as pl
from jax.experimental.pallas import tpu as pltpu
from jax.sharding import Mesh
from jax.sharding import PartitionSpec as P

AXES = ("groups", "z", "y", "c")
BLOCK = 16
LANES = 128
WINDOW = 4
SWAP = [(0, 1), (1, 0)]


def chunks_of(per_plane):
    unit = per_plane // 16
    sizes = [6 * unit, 6 * unit, 4 * unit] if unit else [1] * per_plane
    return [(sum(sizes[:i]), size) for i, size in enumerate(sizes)]


def nt_dot(a, b):
    return lax.dot_general(a, b, (((1,), (1,)), ((), ())), preferred_element_type=jnp.float32)


def tn_dot(a, b):
    return lax.dot_general(a, b, (((0,), (0,)), ((), ())), preferred_element_type=jnp.float32)


def after(value, *others):
    return lax.optimization_barrier((value, others))[0]


def unfold_kernel(planes, per_plane, chunks, extra, z_ref, *refs):
    ins, factor, outs, wide = refs[:planes], refs[planes], refs[planes + 1 : -1], refs[-1]
    rows, _, cells = ins[0].shape
    for shift in range(planes):
        first = lax.rem(lax.rem(z_ref[0] + shift, planes) * per_plane, BLOCK)
        for h in range(0, cells, LANES):
            wide[...] = ins[shift][:, :, h : h + LANES].astype(jnp.float32).reshape(rows * BLOCK, LANES)
            for n, (start, size) in enumerate(chunks):
                out = outs[n * planes + shift]
                for s in range(size):
                    taken = wide[pl.ds(first + start + s, rows, stride=BLOCK), :]
                    out[:, s * cells + h : s * cells + h + LANES] = taken.astype(jnp.bfloat16)
        if extra is not None:
            outs[extra * planes + shift][:, chunks[extra][1] * cells :] = factor[...]


def unfold(slab, factor, z, planes, chunks, extra):
    rows, species, cells = slab.shape
    rank = factor.shape[1]
    per_plane = species // planes
    step = min(rows, 32)
    widths = [size * cells + (rank if n == extra else 0) for n, (_, size) in enumerate(chunks)]
    in_specs = [
        pl.BlockSpec(
            (step, BLOCK, cells),
            lambda i, z_ref, shift=shift: (i, lax.div(lax.rem(z_ref[0] + shift, planes) * per_plane, BLOCK), 0),
        )
        for shift in range(planes)
    ]
    in_specs.append(pl.BlockSpec((step, rank), lambda i, z_ref: (i, 0)))
    out = pl.pallas_call(
        functools.partial(unfold_kernel, planes, per_plane, chunks, extra),
        out_shape=[jax.ShapeDtypeStruct((rows, width), slab.dtype) for width in widths for _ in range(planes)],
        grid_spec=pltpu.PrefetchScalarGridSpec(
            num_scalar_prefetch=1,
            grid=(rows // step,),
            in_specs=in_specs,
            out_specs=[pl.BlockSpec((step, width), lambda i, z_ref: (i, 0)) for width in widths for _ in range(planes)],
            scratch_shapes=[pltpu.VMEM((step * BLOCK, LANES), jnp.float32)],
        ),
        compiler_params=pltpu.CompilerParams(vmem_limit_bytes=24 * 2**20),
        cost_estimate=pl.CostEstimate(
            flops=0, bytes_accessed=planes * rows * (BLOCK * cells + sum(widths)) * 2, transcendentals=0
        ),
        name="unfold",
    )(z.reshape(1).astype(jnp.int32), *([slab] * planes), factor)
    return [out[n * planes : (n + 1) * planes] for n in range(len(chunks))]


def finish_kernel(planes, scale, place_ref, *refs):
    out = refs[-1]
    rows = out.shape[0]
    sums = []
    for pair in range(2):
        own, below, above = refs[3 * pair : 3 * pair + 3]
        sums.append((own[...] + below[...] + above[...]) * scale)

    def block(k, z):
        at = ((k % 2) * planes + z) * rows
        return sums[k // 2][:, at : at + rows]

    for place in range(4):

        @pl.when(place_ref[0] == place)
        def _():
            for z in range(planes):
                pieces = [block(place ^ other, z) for other in range(4)]
                out[:, z * 4 * rows : (z + 1) * 4 * rows] = jnp.concatenate(pieces, axis=1)


def finish(planes, total, place, parts):
    rows = parts[0].shape[0]
    return pl.pallas_call(
        functools.partial(finish_kernel, planes, 1.0 / total),
        out_shape=jax.ShapeDtypeStruct((rows, 4 * planes * rows), jnp.float32),
        in_specs=[pl.BlockSpec(memory_space=pltpu.SMEM)] + [pl.BlockSpec(memory_space=pltpu.VMEM)] * len(parts),
        out_specs=pl.BlockSpec(memory_space=pltpu.VMEM),
        compiler_params=pltpu.CompilerParams(vmem_limit_bytes=24 * 2**20),
        name="finish",
    )(place.reshape(1).astype(jnp.int32), *parts)


def chain(planes, z, sums, up, ahead):
    rows = sums.shape[0] // planes
    got = early = None
    for step in range(1, planes):
        plane = planes - step + z if up else z - planes + step
        sent = lax.dynamic_slice_in_dim(sums, jnp.clip(plane, 0, planes - 1) * rows, rows, 0)
        if got is not None:
            sent = sent + (after(got, *ahead) if step == 3 else got)
        pairs = [(i, i + 1) for i in range(step)] if up else [(planes - 1 - i, planes - 2 - i) for i in range(step)]
        early = sent if step < 3 else early
        got = lax.ppermute(sent, "z", pairs)
    return got, early


def on_device(planes, slab, factor):
    rows, species, cells = slab.shape
    rank = factor.shape[1]
    total = species * cells
    z, y, c = (lax.axis_index(name) for name in ("z", "y", "c"))
    place = y * 2 + c
    per_plane = species // planes
    chunks = chunks_of(per_plane)
    last = len(chunks) - 1
    pieces = unfold(slab, factor, z, planes, chunks[:1], None)
    pieces += unfold(slab, after(factor, pieces[0]), z, planes, chunks[1:], 0)

    def stacked(parts):
        stack = jnp.zeros((planes,) + parts[0].shape, slab.dtype)
        for shift in range(planes):
            stack = lax.dynamic_update_slice(stack, parts[shift][None], ((z - shift) % planes, 0, 0))
        return stack.reshape(planes * rows, -1)

    sent, waits, held = [], [], []
    for j in range(last + 1):
        arrived = [pieces[j][0] if j else after(pieces[0][0], pieces[1])]
        for shift in range(1, planes):
            piece = pieces[j][shift]
            if len(sent) >= WINDOW:
                piece = after(
                    piece,
                    sent[-WINDOW],
                    *(waits[j - 2] if j > 1 else ()),
                )
            sent.append(lax.ppermute(piece, "z", [(s, (s + shift) % planes) for s in range(planes)]))
            arrived.append(sent[-1])
        stack = stacked(arrived)
        across = lax.ppermute(stack, "y", SWAP)
        beside = lax.ppermute(stack, "c", SWAP)
        waits.append((across, beside))
        held.append([stack, beside, across])
        if j < last - 1:
            held[j].append(lax.ppermute(across, "c", SWAP))
    flat = [[b[:, : size * cells] for b in held[j][:2]] for j, (_, size) in enumerate(chunks)]
    sums = [sum(nt_dot(flat[j][0], flat[j][k]) for j in range(last + 1)) for k in range(2)]
    parts, gate = [], None
    for half in range(2):
        if half:
            for j in range(last + 1):
                if j >= last - 1:
                    held[j][2] = after(held[j][2], *gate)
                    held[j].append(lax.ppermute(held[j][2], "c", SWAP))
                flat[j] += [b[:, : chunks[j][1] * cells] for b in held[j][2:]]
            sums = [sum(nt_dot(flat[j][0], flat[j][k]) for j in range(last + 1)) for k in range(2, 4)]
        both = jnp.concatenate(sums, axis=1)
        up, early_up = chain(planes, z, both, True, parts[1:3])
        down, early_down = chain(planes, z, both, False, parts[1:3])
        gate = (early_up, early_down)
        parts += [lax.dynamic_slice_in_dim(both, z * rows, rows, 0), up, down]
    gram = finish(planes, total, place, parts)
    own = per_plane // 4

    def kept(mine, held):
        out = []
        for j, (start, size) in enumerate(chunks):
            low, high = max(start, mine * own) - start, min(start + size, (mine + 1) * own) - start
            if low < high:
                out.append(
                    sum(
                        tn_dot(held[j][k][:, low * cells : high * cells], held[1][k][:, chunks[1][1] * cells :])
                        for k in range(4)
                    )
                )
        return jnp.concatenate(out, axis=0)

    core = lax.switch(place, [functools.partial(kept, mine) for mine in range(4)], after(held, *gate))
    return (gram, core)


def solution(mesh):
    groups, n = mesh.devices.shape
    planes = n // 4
    fine = Mesh(np.reshape(mesh.devices, (groups, planes, 2, 2)), AXES)
    spec = P(AXES)
    return jax.shard_map(
        lambda slab, factor: on_device(planes, slab, factor),
        mesh=fine,
        in_specs=(spec, spec),
        out_specs=(spec, spec),
        check_vma=False,
    )
```

```python
import functools

import jax
import jax.numpy as jnp
import numpy as np
from jax import lax
from jax.experimental import pallas as pl
from jax.experimental.pallas import tpu as pltpu
from jax.sharding import Mesh
from jax.sharding import PartitionSpec as P

AXES = ("groups", "z", "y", "c")
BLOCK = 16
LANES = 128
WINDOW = 6
SWAP = [(0, 1), (1, 0)]


def chunks_of(per_plane):
    unit = per_plane // 16
    sizes = [6 * unit, 6 * unit, 4 * unit] if unit else [1] * per_plane
    return [(sum(sizes[:i]), size) for i, size in enumerate(sizes)]


def nt_dot(a, b):
    return lax.dot_general(a, b, (((1,), (1,)), ((), ())), preferred_element_type=jnp.float32)


def tn_dot(a, b):
    return lax.dot_general(a, b, (((0,), (0,)), ((), ())), preferred_element_type=jnp.float32)


def after(value, *others):
    return lax.optimization_barrier((value, others))[0]


def unfold_kernel(planes, per_plane, chunks, extra, z_ref, *refs):
    ins, factor, outs, wide = refs[:planes], refs[planes], refs[planes + 1 : -1], refs[-1]
    rows, _, cells = ins[0].shape
    for shift in range(planes):
        first = lax.rem(lax.rem(z_ref[0] + shift, planes) * per_plane, BLOCK)
        for h in range(0, cells, LANES):
            wide[...] = ins[shift][:, :, h : h + LANES].astype(jnp.float32).reshape(rows * BLOCK, LANES)
            for n, (start, size) in enumerate(chunks):
                out = outs[n * planes + shift]
                for s in range(size):
                    taken = wide[pl.ds(first + start + s, rows, stride=BLOCK), :]
                    out[:, s * cells + h : s * cells + h + LANES] = taken.astype(jnp.bfloat16)
        if extra is not None:
            outs[extra * planes + shift][:, chunks[extra][1] * cells :] = factor[...]


def unfold(slab, factor, z, planes, chunks, extra):
    rows, species, cells = slab.shape
    rank = factor.shape[1]
    per_plane = species // planes
    step = min(rows, 32)
    widths = [size * cells + (rank if n == extra else 0) for n, (_, size) in enumerate(chunks)]
    in_specs = [
        pl.BlockSpec(
            (step, BLOCK, cells),
            lambda i, z_ref, shift=shift: (i, lax.div(lax.rem(z_ref[0] + shift, planes) * per_plane, BLOCK), 0),
        )
        for shift in range(planes)
    ]
    in_specs.append(pl.BlockSpec((step, rank), lambda i, z_ref: (i, 0)))
    out = pl.pallas_call(
        functools.partial(unfold_kernel, planes, per_plane, chunks, extra),
        out_shape=[jax.ShapeDtypeStruct((rows, width), slab.dtype) for width in widths for _ in range(planes)],
        grid_spec=pltpu.PrefetchScalarGridSpec(
            num_scalar_prefetch=1,
            grid=(rows // step,),
            in_specs=in_specs,
            out_specs=[pl.BlockSpec((step, width), lambda i, z_ref: (i, 0)) for width in widths for _ in range(planes)],
            scratch_shapes=[pltpu.VMEM((step * BLOCK, LANES), jnp.float32)],
        ),
        compiler_params=pltpu.CompilerParams(vmem_limit_bytes=24 * 2**20),
        cost_estimate=pl.CostEstimate(
            flops=0, bytes_accessed=planes * rows * (BLOCK * cells + sum(widths)) * 2, transcendentals=0
        ),
        name="unfold",
    )(z.reshape(1).astype(jnp.int32), *([slab] * planes), factor)
    return [out[n * planes : (n + 1) * planes] for n in range(len(chunks))]


def finish_kernel(planes, scale, place_ref, *refs):
    out = refs[-1]
    rows = out.shape[0]
    sums = []
    for pair in range(2):
        own, below, above = refs[3 * pair : 3 * pair + 3]
        sums.append((own[...] + below[...] + above[...]) * scale)

    def block(k, z):
        at = ((k % 2) * planes + z) * rows
        return sums[k // 2][:, at : at + rows]

    for place in range(4):

        @pl.when(place_ref[0] == place)
        def _():
            for z in range(planes):
                pieces = [block(place ^ other, z) for other in range(4)]
                out[:, z * 4 * rows : (z + 1) * 4 * rows] = jnp.concatenate(pieces, axis=1)


def finish(planes, total, place, parts):
    rows = parts[0].shape[0]
    return pl.pallas_call(
        functools.partial(finish_kernel, planes, 1.0 / total),
        out_shape=jax.ShapeDtypeStruct((rows, 4 * planes * rows), jnp.float32),
        in_specs=[pl.BlockSpec(memory_space=pltpu.SMEM)] + [pl.BlockSpec(memory_space=pltpu.VMEM)] * len(parts),
        out_specs=pl.BlockSpec(memory_space=pltpu.VMEM),
        compiler_params=pltpu.CompilerParams(vmem_limit_bytes=24 * 2**20),
        name="finish",
    )(place.reshape(1).astype(jnp.int32), *parts)


def chain(planes, z, sums, up):
    rows = sums.shape[0] // planes
    got = first = None
    for step in range(1, planes):
        plane = planes - step + z if up else z - planes + step
        sent = lax.dynamic_slice_in_dim(sums, jnp.clip(plane, 0, planes - 1) * rows, rows, 0)
        if got is not None:
            sent = sent + got
        pairs = [(i, i + 1) for i in range(step)] if up else [(planes - 1 - i, planes - 2 - i) for i in range(step)]
        got = lax.ppermute(sent, "z", pairs)
        first = got if first is None else first
    return got, first


def on_device(planes, slab, factor):
    rows, species, cells = slab.shape
    rank = factor.shape[1]
    total = species * cells
    z, y, c = (lax.axis_index(name) for name in ("z", "y", "c"))
    place = y * 2 + c
    per_plane = species // planes
    chunks = chunks_of(per_plane)
    last = len(chunks) - 1
    pieces = unfold(slab, factor, z, planes, chunks[:1], None)
    pieces += unfold(slab, after(factor, pieces[0]), z, planes, chunks[1:], 0)

    def stacked(parts):
        stack = jnp.zeros((planes,) + parts[0].shape, slab.dtype)
        for shift in range(planes):
            stack = lax.dynamic_update_slice(stack, parts[shift][None], ((z - shift) % planes, 0, 0))
        return stack.reshape(planes * rows, -1)

    sent, waits, held = [], [], []
    for j in range(last + 1):
        arrived = [pieces[j][0] if j else after(pieces[0][0], pieces[1])]
        for shift in range(1, planes):
            piece = pieces[j][shift]
            if len(sent) >= WINDOW:
                piece = after(
                    piece,
                    sent[-WINDOW],
                    *(waits[j - 2] if j > 1 else ()),
                )
            sent.append(lax.ppermute(piece, "z", [(s, (s + shift) % planes) for s in range(planes)]))
            arrived.append(sent[-1])
        stack = stacked(arrived)
        across = lax.ppermute(stack, "y", SWAP)
        beside = lax.ppermute(stack, "c", SWAP)
        waits.append((across, beside))
        held.append([stack, beside, across])
        if j < last:
            held[j].append(lax.ppermute(across, "c", SWAP))
    flat = [[b[:, : size * cells] for b in held[j][:2]] for j, (_, size) in enumerate(chunks)]
    sums = [sum(nt_dot(flat[j][0], flat[j][k]) for j in range(last + 1)) for k in range(2)]
    parts, gate = [], None
    for half in range(2):
        if half:
            for j in range(last + 1):
                if j == last:
                    held[j][2] = after(held[j][2], *gate)
                    held[j].append(lax.ppermute(held[j][2], "c", SWAP))
                flat[j] += [b[:, : chunks[j][1] * cells] for b in held[j][2:]]
            sums = [sum(nt_dot(flat[j][0], flat[j][k]) for j in range(last + 1)) for k in range(2, 4)]
        both = jnp.concatenate(sums, axis=1)
        up, first_up = chain(planes, z, both, True)
        down, first_down = chain(planes, z, both, False)
        gate = (first_up, first_down)
        parts += [lax.dynamic_slice_in_dim(both, z * rows, rows, 0), up, down]
    gram = finish(planes, total, place, parts)
    own = per_plane // 4

    def kept(mine, held):
        out = []
        for j, (start, size) in enumerate(chunks):
            low, high = max(start, mine * own) - start, min(start + size, (mine + 1) * own) - start
            if low < high:
                out.append(
                    sum(
                        tn_dot(held[j][k][:, low * cells : high * cells], held[1][k][:, chunks[1][1] * cells :])
                        for k in range(4)
                    )
                )
        return jnp.concatenate(out, axis=0)

    core = lax.switch(place, [functools.partial(kept, mine) for mine in range(4)], after(held, *gate))
    return (gram, core)


def solution(mesh):
    groups, n = mesh.devices.shape
    planes = n // 4
    fine = Mesh(np.reshape(mesh.devices, (groups, planes, 2, 2)), AXES)
    spec = P(AXES)
    return jax.shard_map(
        lambda slab, factor: on_device(planes, slab, factor),
        mesh=fine,
        in_specs=(spec, spec),
        out_specs=(spec, spec),
        check_vma=False,
    )
```
